256 devices in a mesh: row: 32 (over z, x), col: 8 (over y, core).
Axes of the slice: x: 4, y: 4, z: 8, core: 2. Of those that a mesh axis runs over, the one named last changes fastest.
Arguments:
- solution_field: float32 [32, 262144], P(None, ('row', 'col')), may hold values from -6 to 6
- residual: float32 [32, 262144], P(None, ('row', 'col')), may hold values from -420 to 420
- direction: float32 [32, 262144], P(None, ('row', 'col')), may hold values from -420 to 420
- positions: bfloat16 [2, 262144], P(None, ('row', 'col')), may hold values from -6 to 6
- tile_pairs: int32 [2, 393216], P(None, ('row', 'col')), may hold values from 0 to 255, as said below
- pair_count: int32 [256], P(('row', 'col')), may hold values from 0 to 1536, as said below
Outputs:
- solution_next: float32 [32, 262144], P(None, ('row', 'col'))
- residual_next: float32 [32, 262144], P(None, ('row', 'col'))
- direction_next: float32 [32, 262144], P(None, ('row', 'col'))
The draws below stay inside these ranges and needn't reach their ends.
Inputs may be any that keep to these rules, and one draw needn't show every extreme that they name: `tile_pairs`: row 0 holds local row tiles below 64, row 1 local column tiles below 256. The live pairs of one slot block are distinct and strictly upper (I < J); entries in slots that are not live are in range but carry nothing. `pair_count`: some slot block is full in every draw.
All inputs are finite; a program needn't handle non-finite values.
Results may differ from the reference program's by a relative error of at most 0.007.
Values may be sent and summed in bfloat16 or wider, within the bound.
No kernel may reach another device: no remote copies, remote signals or barrier semaphores. Data moves between devices by JAX's collectives and lax.ppermute only.
A program may use at most 64 MiB of HBM per device.

```python
import math
import jax
import jax.numpy as jnp
from jax import lax

TILE = 128
PROBES = 32
TILE_DEV = 8
PAIRS_DEV = 1536
NPTS = 262144
N_ROW = 32
N_COL = 8
DEVICES = 256


def pattern_draw(key):
    key_pick = jax.random.fold_in(key, 11)
    key_rank = jax.random.fold_in(key, 12)
    key_full = jax.random.fold_in(key, 13)
    row_span = N_COL * TILE_DEV
    col_span = N_ROW * TILE_DEV
    device = jnp.arange(DEVICES, dtype=jnp.int32)
    row_dev = device // N_COL
    col_dev = device % N_COL
    row_tile = row_dev[:, None] * row_span + jnp.arange(row_span, dtype=jnp.int32)[None, :]
    col_local = jnp.arange(col_span, dtype=jnp.int32)
    col_tile = (col_local[None, :] // TILE_DEV * N_COL + col_dev[:, None]) * TILE_DEV + col_local[None, :] % TILE_DEV
    cell_total = row_span * col_span
    upper_mask = (row_tile[:, :, None] < col_tile[:, None, :]).reshape(DEVICES, cell_total)
    upper_count = jnp.sum(upper_mask.astype(jnp.int32), axis=1)
    levels = jax.random.randint(key_pick, (DEVICES,), 0, 3)
    full_device = jax.random.randint(key_full, (), 0, N_COL)
    levels = jnp.where(device == full_device, 0, levels)
    divisor = jnp.where(levels == 0, 1, jnp.where(levels == 1, 8, 64))
    counts = jnp.minimum(PAIRS_DEV, upper_count // divisor).astype(jnp.int32)
    spread = max(1, 2 ** 30 // cell_total)
    cell_index = jnp.arange(cell_total, dtype=jnp.int32)[None, :]
    scores = jax.random.randint(key_rank, (DEVICES, cell_total), 0, spread) * cell_total + cell_index
    scores = jnp.where(upper_mask, scores, -1 - cell_index)
    ranked, chosen = lax.top_k(scores, PAIRS_DEV)
    pair_table = jnp.stack([chosen // col_span, chosen % col_span]).reshape(2, DEVICES * PAIRS_DEV)
    return (pair_table.astype(jnp.int32), counts)


def draw_tile_pairs(key, part):
    return pattern_draw(key)[0]


def draw_pair_count(key, part):
    return pattern_draw(key)[1]


def probe_draw(key):
    base_part = jnp.clip(jax.random.normal(jax.random.fold_in(key, 21), (PROBES, NPTS), jnp.float32), -5.0, 5.0)
    noise_part = jnp.clip(jax.random.normal(jax.random.fold_in(key, 22), (PROBES, NPTS), jnp.float32), -5.0, 5.0)
    return (base_part, base_part + 0.6 * noise_part)


def draw_residual(key, part):
    return probe_draw(key)[0]


def draw_direction(key, part):
    return probe_draw(key)[1]


def level_of(key, dims, pieces, low, top_value):
    level = 1.0
    for dim, shards_of in pieces:
        steps = jax.random.uniform(jax.random.fold_in(jax.random.fold_in(key, 6), dim), (shards_of,), jnp.float32, low / len(pieces), top_value / len(pieces))
        level = level * jnp.repeat(jnp.exp(steps), dims[dim] // shards_of).reshape((-1,) + (1,) * (len(dims) - 1 - dim))
    return level


def normal_values(key, dims, scale, most, shards=(), kind=jnp.bfloat16):
    level = level_of(key, dims, shards, -0.22, 0.18) if shards else 1.0
    result = jax.random.normal(key, dims, jnp.float32) * scale * level
    return jnp.minimum(jnp.maximum(result, -most), most).astype(kind)


def setup_inputs(seed: int = 0) -> dict:
    key_list = jax.random.split(jax.random.key(seed), 7)
    return {
        "solution_field": normal_values(key_list[0], (PROBES, NPTS), 1.0, 6.0, ((1, 256),), jnp.float32),
        "residual": draw_residual(jax.random.fold_in(key_list[6], 71), 0),
        "direction": draw_direction(jax.random.fold_in(key_list[6], 71), 0),
        "positions": normal_values(key_list[3], (2, NPTS), 1.0, 6.0, ((1, 256),)),
        "tile_pairs": draw_tile_pairs(jax.random.fold_in(key_list[6], 71), 0),
        "pair_count": draw_pair_count(jax.random.fold_in(key_list[6], 71), 0),
    }


AMPLITUDE = 0.025
NUGGET = 2.0
RADIUS = 1.0
HIGHEST = lax.Precision.HIGHEST

def kernel_tile(near_side, far_side):
    differ = near_side[..., :, None] - far_side[..., None, :]
    distance = jnp.sqrt(lax.optimization_barrier(jnp.sum(differ * differ, axis=0))) / RADIUS
    remain = jnp.maximum(1.0 - distance, 0.0)
    return AMPLITUDE * remain ** 4 * (4.0 * distance + 1.0)

def cross_gram_matrix(former, latter):
    return lax.dot_general(former.astype(jnp.float32), latter.astype(jnp.float32), (((1,), (1,)), ((), ())), precision=HIGHEST, preferred_element_type=jnp.float32)

def apply_left(matrix, vectors):
    return jnp.dot(matrix.T, vectors, precision=HIGHEST)

def symmetric_solve(matrix, target):
    balanced = 0.5 * (matrix + matrix.T)
    factor = jnp.linalg.cholesky(balanced)
    middle = lax.linalg.triangular_solve(factor, target, left_side=True, lower=True)
    return lax.linalg.triangular_solve(factor, middle, left_side=True, lower=True, transpose_a=True)

def reference(solution_field, residual, direction, positions, tile_pairs, pair_count):
    tile_count = NPTS // TILE
    dir_half = lax.optimization_barrier(direction.astype(jnp.bfloat16))
    dir_round = dir_half.astype(jnp.float32).reshape(PROBES, tile_count, TILE)
    coords = positions.astype(jnp.float32).reshape(2, tile_count, TILE)
    total = DEVICES * PAIRS_DEV
    entry = jnp.arange(total, dtype=jnp.int32)
    device = entry // PAIRS_DEV
    slot_index = entry % PAIRS_DEV
    row_dev = device // N_COL
    col_dev = device % N_COL
    row_tile = (row_dev * (N_COL * TILE_DEV) + tile_pairs[0]).astype(jnp.int32)
    col_local = tile_pairs[1]
    col_tile = ((col_local // TILE_DEV * N_COL + col_dev) * TILE_DEV + col_local % TILE_DEV).astype(jnp.int32)
    live_mask = slot_index < pair_count[device]
    block_size = math.gcd(total, 256)
    block_count = total // block_size

    def accumulate(running_totals, packed):
        rows_now, cols_now, live_now = packed
        kernel_block = kernel_tile(coords[:, rows_now], coords[:, cols_now])
        kernel_block = jnp.where(live_now[:, None, None], kernel_block, 0.0).astype(jnp.bfloat16)
        kernel_block = lax.optimization_barrier(kernel_block).astype(jnp.float32)
        forward_step = jnp.einsum('bpq,kbq->kbp', kernel_block, dir_round[:, cols_now], precision=HIGHEST)
        backward = jnp.einsum('bpq,kbp->kbq', kernel_block, dir_round[:, rows_now], precision=HIGHEST)
        running_totals = running_totals.at[:, rows_now].add(forward_step)
        running_totals = running_totals.at[:, cols_now].add(backward)
        return (running_totals, None)
    packed = (row_tile.reshape(block_count, block_size), col_tile.reshape(block_count, block_size), live_mask.reshape(block_count, block_size))
    kernel_sum, unused = lax.scan(accumulate, jnp.zeros((PROBES, tile_count, TILE), jnp.float32), packed)
    diagonal = lax.optimization_barrier(kernel_tile(coords, coords).astype(jnp.bfloat16)).astype(jnp.float32)
    kernel_sum = kernel_sum + jnp.einsum('npq,knq->knp', diagonal, dir_round, precision=HIGHEST)
    applied = NUGGET * direction + kernel_sum.reshape(PROBES, NPTS)
    curvature = cross_gram_matrix(direction, applied)
    crossing = cross_gram_matrix(direction, residual)
    norm_old = cross_gram_matrix(residual, residual)
    step_size = symmetric_solve(curvature, crossing)
    solution_next = solution_field + apply_left(step_size, direction)
    residual_next = residual - apply_left(step_size, applied)
    norm_new = cross_gram_matrix(residual_next, residual_next)
    mix_weight = symmetric_solve(norm_old, norm_new)
    direction_next = residual_next + apply_left(mix_weight, direction)
    return (solution_next, residual_next, direction_next)
```

```python
import functools

import jax
import jax.numpy as jnp
import numpy as np
from jax import lax
from jax.experimental import pallas as pl
from jax.experimental.pallas import tpu as pltpu
from jax.sharding import Mesh
from jax.sharding import PartitionSpec as P

TILE = 128
PROBES = 32
UNROLL = 16
NUGGET = 2.0
KERNEL_SCALE = 0.1
HIGHEST = lax.Precision.HIGHEST
f32, bf16 = jnp.float32, jnp.bfloat16
VMEM = pl.BlockSpec(memory_space=pltpu.VMEM)
SMEM = pl.BlockSpec(memory_space=pltpu.SMEM)
NT = (((1,), (1,)), ((), ()))
NN = (((1,), (0,)), ((), ()))
TN = (((0,), (0,)), ((), ()))
PARAMS = pltpu.CompilerParams(vmem_limit_bytes=48 * 2**20)


def pack_kernel(direction_ref, positions_ref, packed_ref):
    for t in range(8):
        packed_ref[t * 32 : (t + 1) * 32, :] = direction_ref[:, t * TILE : (t + 1) * TILE].astype(bf16)
    where = positions_ref[...].astype(f32)
    rows = [where[d : d + 1, t * TILE : (t + 1) * TILE] for d in range(2) for t in range(8)]
    packed_ref[256:272, :] = jnp.concatenate(rows, 0).astype(bf16)


def radial(square):
    distance = pl.reciprocal(lax.rsqrt(square), approx=True)
    remain = jnp.maximum(1.0 - distance, 0.0)
    remain2 = remain * remain
    return ((remain2 * remain2) * (1.25 - remain)).astype(bf16)


def pair_kernel(place_ref, pairs_ref, own_ref, row_ref, col_ref, row_out, col_out, own_out, px, py, qx, qy, row_acc, col_acc):
    live, y_own, core_own = place_ref[0], place_ref[1], place_ref[2]
    row_acc[...] = jnp.zeros_like(row_acc)
    col_acc[...] = jnp.zeros_like(col_acc)

    def col_prepare(r, carry):
        where = col_ref[r, 256:272, :].astype(f32)
        for t in range(8):
            qx[r * 8 + t] = jnp.broadcast_to(where[t : t + 1], (8, TILE))
            qy[r * 8 + t] = jnp.broadcast_to(where[8 + t : 9 + t], (8, TILE))
        return carry

    lax.fori_loop(0, 32, col_prepare, 0)

    def spread(line):
        return jnp.broadcast_to(line, (TILE, TILE)).T

    def row_prepare(r, carry):
        where = row_ref[r, 256:272, :].astype(f32)
        for t in range(8):
            px[r * 8 + t] = spread(where[t : t + 1])
            py[r * 8 + t] = spread(where[8 + t : 9 + t])
        return carry

    lax.fori_loop(0, 8, row_prepare, 0)

    where = own_ref[256:272, :].astype(f32)
    for t in range(8):
        dx = spread(where[t : t + 1]) - where[t : t + 1]
        dy = spread(where[8 + t : 9 + t]) - where[8 + t : 9 + t]
        block = radial(dx * dx + dy * dy)
        own_out[:, t * TILE : (t + 1) * TILE] = KERNEL_SCALE * lax.dot_general(
            own_ref[t * 32 : (t + 1) * 32, :], block, NT, preferred_element_type=f32
        )

    def body(i, carry):
        results = []
        for u in range(UNROLL):
            e = i * UNROLL + u
            a, b = pairs_ref[0, e], pairs_ref[1, e]
            keep = jnp.where(e < live, 1.0, 0.0).astype(bf16)
            shift = (y_own - (a >> 4)) & 3
            slot = shift + 4 * (((a >> 3) & 1) ^ core_own)
            tile = slot * 8 + (a & 7)
            near = row_ref[slot, pl.ds(pl.multiple_of((a & 7) * 32, 32), 32), :] * keep
            far = col_ref[b >> 3, pl.ds(pl.multiple_of((b & 7) * 32, 32), 32), :] * keep
            dx = px[tile].reshape(16, 8, TILE) - qx[b][None]
            dy = py[tile].reshape(16, 8, TILE) - qy[b][None]
            block = radial((dx * dx + dy * dy).reshape(TILE, TILE))
            forward = lax.dot_general(far, block, NT, preferred_element_type=f32)
            backward = lax.dot_general(near, block, NN, preferred_element_type=f32)
            results.append((tile, b, forward, backward))
        for tile, b, forward, backward in results:
            row_acc[tile] += forward
            col_acc[b] += backward
        return carry

    lax.fori_loop(0, (live + UNROLL - 1) // UNROLL, body, 0)

    def finish(out, acc):
        def step(r, carry):
            for t in range(8):
                out[r, t * 32 : (t + 1) * 32, :] = (KERNEL_SCALE * acc[r * 8 + t]).astype(bf16)
            return carry

        lax.fori_loop(0, out.shape[0], step, 0)

    finish(row_out, row_acc)
    finish(col_out, col_acc)


def dot32(former, latter, dims):
    return lax.dot_general(former, latter, dims, precision=HIGHEST, preferred_element_type=f32)


def gram_kernel(direction_ref, residual_ref, own_ref, row_ref, col_ref, image_ref, gram_ref):
    for t in range(8):
        here = slice(t * 32, (t + 1) * 32)
        lanes = slice(t * TILE, (t + 1) * TILE)
        total = NUGGET * direction_ref[:, lanes] + own_ref[:, lanes]
        for part in range(row_ref.shape[0]):
            total = total + row_ref[part, here, :].astype(f32)
        for part in range(col_ref.shape[0]):
            total = total + col_ref[part, here, :].astype(f32)
        image_ref[:, lanes] = total
    direction, residual, image = direction_ref[...], residual_ref[...], image_ref[...]
    gram_ref[0:32, 0:32] = dot32(direction, image, NT)
    gram_ref[0:32, 32:64] = dot32(direction, residual, NT)
    gram_ref[0:32, 64:96] = dot32(residual, residual, NT)
    gram_ref[0:32, 96:128] = dot32(residual, image, NT)
    square = dot32(image, image, NT)
    for t in range(4):
        gram_ref[32:40, t * 32 : (t + 1) * 32] = square[t * 8 : (t + 1) * 8]


def solve_kernel(gram_ref, solution_ref, residual_ref, direction_ref, image_ref, solution_out, residual_out, direction_out):
    gram = gram_ref[...]
    curvature, crossing = gram[0:32, 0:32], gram[0:32, 32:64]
    norm_old, mixed = gram[0:32, 64:96], gram[0:32, 96:128]
    square = jnp.concatenate([gram[32:40, t * 32 : (t + 1) * 32] for t in range(4)], 0)
    row = lax.broadcasted_iota(jnp.int32, (32, 64), 0)
    lane = lax.broadcasted_iota(jnp.int32, (32, 64), 1)
    unit = jnp.where(row[:, :32] == lane[:, :32], 1.0, 0.0).astype(f32)
    first = jnp.concatenate([0.5 * (curvature + curvature.T), crossing], 1)
    second = jnp.concatenate([0.5 * (norm_old + norm_old.T), unit], 1)

    def eliminate(table, k):
        pivot_row = table[k : k + 1, :] / table[k : k + 1, k : k + 1]
        return jnp.where(row == k, pivot_row, table - table[:, k : k + 1] * pivot_row)

    for k in range(32):
        first, second = eliminate(first, k), eliminate(second, k)
    alpha, inverse = first[:, 32:64], second[:, 32:64]
    cross = dot32(mixed, alpha, NN)
    norm_new = 0.5 * (norm_old + norm_old.T) - cross - cross.T + dot32(alpha, dot32(square, alpha, NN), TN)
    beta = dot32(inverse, norm_new, NN)
    direction = direction_ref[...]
    residual_next = residual_ref[...] - dot32(alpha, image_ref[...], TN)
    residual_out[...] = residual_next
    solution_out[...] = solution_ref[...] + dot32(alpha, direction, TN)
    direction_out[...] = residual_next + dot32(beta, direction, TN)


def shifts(value, axis, size):
    return [lax.ppermute(value, axis, [(i, (i + k) % size) for i in range(size)]) for k in range(1, size)]


def swap(value):
    return lax.ppermute(value, "core", [(0, 1), (1, 0)])


def on_device(solution_field, residual, direction, positions, tile_pairs, pair_count):
    shape = jax.ShapeDtypeStruct
    own_points = direction.shape[1]
    y_own, core_own = lax.axis_index("y"), lax.axis_index("core")
    packed = pl.pallas_call(
        pack_kernel, out_shape=shape((272, TILE), bf16), in_specs=[VMEM] * 2, out_specs=VMEM, name="pack"
    )(direction, positions)
    row_half = jnp.stack([packed] + shifts(packed, "y", 4))
    row_all = jnp.concatenate([row_half, swap(row_half)], 0)
    col_all = lax.all_gather(lax.all_gather(packed, "x"), "z").reshape(32, 272, TILE)
    place = jnp.stack([pair_count[0], y_own, core_own]).astype(jnp.int32)
    row_sum, col_sum, own_product = pl.pallas_call(
        pair_kernel,
        out_shape=(shape((8, 256, TILE), bf16), shape((32, 256, TILE), bf16), shape((PROBES, own_points), f32)),
        in_specs=[SMEM, SMEM, VMEM, VMEM, VMEM],
        out_specs=(VMEM, VMEM, VMEM),
        scratch_shapes=[
            pltpu.VMEM((64, TILE, TILE), f32),
            pltpu.VMEM((64, TILE, TILE), f32),
            pltpu.VMEM((256, 8, TILE), f32),
            pltpu.VMEM((256, 8, TILE), f32),
            pltpu.VMEM((64, PROBES, TILE), f32),
            pltpu.VMEM((256, PROBES, TILE), f32),
        ],
        compiler_params=PARAMS,
        name="pairs",
    )(place, tile_pairs, packed, row_all, col_all)
    half = row_sum[:4].astype(f32) + swap(row_sum[4:]).astype(f32)
    half = half.astype(bf16)
    row_parts = [half[0]] + [
        lax.ppermute(half[k], "y", [(i, (i - k) % 4) for i in range(4)]) for k in range(1, 4)
    ]
    row_parts = jnp.stack(row_parts)
    col_parts = lax.all_to_all(col_sum, ("z", "x"), 0, 0)
    image, gram = pl.pallas_call(
        gram_kernel,
        out_shape=(shape((PROBES, own_points), f32), shape((40, TILE), f32)),
        in_specs=[VMEM] * 5,
        out_specs=(VMEM, VMEM),
        compiler_params=PARAMS,
        name="gram",
    )(direction, residual, own_product, row_parts, col_parts)
    gram = gram + swap(gram)
    for axis, size in (("y", 4), ("x", 4), ("z", 8)):
        gram = sum(shifts(gram, axis, size), gram)
    return pl.pallas_call(
        solve_kernel,
        out_shape=(shape((PROBES, own_points), f32),) * 3,
        in_specs=[VMEM] * 5,
        out_specs=(VMEM,) * 3,
        compiler_params=PARAMS,
        name="solve",
    )(gram, solution_field, residual, direction, image)


def solution(mesh):
    fine = Mesh(np.asarray(mesh.devices).reshape(8, 4, 4, 2), ("z", "x", "y", "core"))
    points = P(None, ("z", "x", "y", "core"))
    return jax.shard_map(
        on_device,
        mesh=fine,
        in_specs=(points,) * 5 + (P(("z", "x", "y", "core")),),
        out_specs=(points,) * 3,
        check_vma=False,
    )
```

```python
import functools

import jax
import jax.numpy as jnp
import numpy as np
from jax import lax
from jax.experimental import pallas as pl
from jax.experimental.pallas import tpu as pltpu
from jax.sharding import Mesh
from jax.sharding import PartitionSpec as P

TILE = 128
PROBES = 32
UNROLL = 32
TAIL = 8
PARTS = 4
BIN = 1536 + UNROLL
NUGGET = 2.0
KERNEL_SCALE = 0.1
HIGHEST = lax.Precision.HIGHEST
f32, bf16 = jnp.float32, jnp.bfloat16
VMEM = pl.BlockSpec(memory_space=pltpu.VMEM)
SMEM = pl.BlockSpec(memory_space=pltpu.SMEM)
NT = (((1,), (1,)), ((), ()))
NN = (((1,), (0,)), ((), ()))
TN = (((0,), (0,)), ((), ()))
PARAMS = pltpu.CompilerParams(vmem_limit_bytes=16 * 2**20)


def cost(microseconds):
    return pl.CostEstimate(flops=0, bytes_accessed=int(microseconds * 3_500_000), transcendentals=0)


def pack_kernel(direction_ref, positions_ref, packed_ref):
    where = positions_ref[...].astype(f32)
    for h in range(2):
        for t in range(4):
            lanes = slice((h * 4 + t) * TILE, (h * 4 + t + 1) * TILE)
            packed_ref[h * 144 + t * 32 : h * 144 + (t + 1) * 32, :] = direction_ref[:, lanes].astype(bf16)
        rows = [where[d : d + 1, (h * 4 + t) * TILE : (h * 4 + t + 1) * TILE] for d in range(2) for t in range(4)]
        rows.append(jnp.zeros((8, TILE), f32))
        packed_ref[h * 144 + 128 : h * 144 + 144, :] = jnp.concatenate(rows, 0).astype(bf16)


def radial(square):
    distance = pl.reciprocal(lax.rsqrt(square), approx=True)
    remain = jnp.maximum(1.0 - distance, 0.0)
    remain2 = remain * remain
    return ((remain2 * remain2) * (1.25 - remain)).astype(bf16)


def bin_kernel(place_ref, pairs_ref, bins_ref, count_ref):
    live, y_own, core_own = place_ref[0], place_ref[1], place_ref[2]

    def step(e, ends):
        a, b = pairs_ref[0, e], pairs_ref[1, e]
        shift = (y_own - (a >> 4)) & 3
        slot = shift + 4 * (((a >> 3) & 1) ^ core_own)
        tile = slot * 8 + (a & 7)
        part = (b >> 1) & 3
        far = ((b >> 3) << 1) + (b & 1)
        end = jnp.where(part < 2, jnp.where(part == 0, ends[0], ends[1]), jnp.where(part == 2, ends[2], ends[3]))
        bins_ref[part * BIN + end] = tile + (far << 8)
        return tuple(ends[p] + (part == p).astype(jnp.int32) for p in range(PARTS))

    ends = lax.fori_loop(0, live, step, (jnp.int32(0),) * PARTS)
    for p in range(PARTS):
        count_ref[p] = ends[p]
        for j in range(UNROLL):
            bins_ref[p * BIN + ends[p] + j] = 0


def spread(line):
    return jnp.broadcast_to(line, (TILE, TILE)).T


def row_kernel(own_ref, row_ref, px, py, near_out, own_out):
    def step(r, carry):
        for h in range(2):
            where = row_ref[r, h * 144 + 128 : h * 144 + 144, :].astype(f32)
            for t in range(4):
                px[r * 8 + h * 4 + t] = spread(where[t : t + 1])
                py[r * 8 + h * 4 + t] = spread(where[4 + t : 5 + t])
                near_out[r * 8 + h * 4 + t] = row_ref[r, h * 144 + t * 32 : h * 144 + (t + 1) * 32, :]
        return carry

    lax.fori_loop(0, 8, step, 0)
    for h in range(2):
        where = own_ref[h * 144 + 128 : h * 144 + 144, :].astype(f32)
        for t in range(4):
            dx = spread(where[t : t + 1]) - where[t : t + 1]
            dy = spread(where[4 + t : 5 + t]) - where[4 + t : 5 + t]
            block = radial(dx * dx + dy * dy)
            own = own_ref[h * 144 + t * 32 : h * 144 + (t + 1) * 32, :]
            own_out[:, (h * 4 + t) * TILE : (h * 4 + t + 1) * TILE] = KERNEL_SCALE * lax.dot_general(
                own, block, NT, preferred_element_type=f32
            )


def part_kernel(part, *refs):
    if part == 0:
        count_ref, bins_ref, px, py, near_ref, col_ref, row_acc, col_out, qx, qy, col_acc = refs
        row_acc[...] = jnp.zeros_like(row_acc)
    elif part < PARTS - 1:
        count_ref, bins_ref, px, py, near_ref, col_ref, unused, row_acc, col_out, qx, qy, col_acc = refs
    else:
        count_ref, bins_ref, px, py, near_ref, col_ref, row_acc, row_out, col_out, qx, qy, col_acc = refs
    first = part % 2 * 2
    live = count_ref[part]
    col_acc[...] = jnp.zeros_like(col_acc)

    def col_prepare(r, carry):
        where = col_ref[r, 128:144, :].astype(f32)
        for t in range(2):
            qx[r * 2 + t] = jnp.broadcast_to(where[first + t : first + t + 1], (8, TILE))
            qy[r * 2 + t] = jnp.broadcast_to(where[4 + first + t : 5 + first + t], (8, TILE))
        return carry

    lax.fori_loop(0, 32, col_prepare, 0)

    def several(start, number):
        results = []
        for u in range(number):
            e = start + u
            both = bins_ref[part * BIN + e]
            a, b = both & 255, both >> 8
            keep = jnp.where(e < live, 1.0, 0.0).astype(bf16)
            near = near_ref[a] * keep
            far = col_ref[b >> 1, pl.ds(pl.multiple_of((first + (b & 1)) * 32, 32), 32), :] * keep
            dx = px[a].reshape(16, 8, TILE) - qx[b][None]
            dy = py[a].reshape(16, 8, TILE) - qy[b][None]
            block = radial((dx * dx + dy * dy).reshape(TILE, TILE))
            forward = lax.dot_general(far, block, NT, preferred_element_type=f32)
            backward = lax.dot_general(near, block, NN, preferred_element_type=f32)
            results.append((a, b, forward, backward))
        for a, b, forward, backward in results:
            row_acc[a] += forward
            col_acc[b] += backward

    def body(i, carry):
        several(i * UNROLL, UNROLL)
        return carry

    def tail(i, carry):
        several(whole * UNROLL + i * TAIL, TAIL)
        return carry

    whole = live // UNROLL
    lax.fori_loop(0, whole, body, 0)
    lax.fori_loop(0, (live - whole * UNROLL + TAIL - 1) // TAIL, tail, 0)

    def finish(r, carry):
        for t in range(2):
            col_out[r, t * 32 : (t + 1) * 32, :] = (KERNEL_SCALE * col_acc[r * 2 + t]).astype(bf16)
        return carry

    lax.fori_loop(0, 32, finish, 0)
    if part == PARTS - 1:

        def finish_row(r, carry):
            for t in range(8):
                row_out[r, t * 32 : (t + 1) * 32, :] = (KERNEL_SCALE * row_acc[r * 8 + t]).astype(bf16)
            return carry

        lax.fori_loop(0, 8, finish_row, 0)


def dot32(former, latter, dims):
    return lax.dot_general(former, latter, dims, precision=HIGHEST, preferred_element_type=f32)


def gram_kernel(direction_ref, residual_ref, own_ref, row_ref, col_ref, image_ref, gram_ref):
    for t in range(8):
        here = slice(t * 32, (t + 1) * 32)
        lanes = slice(t * TILE, (t + 1) * TILE)
        total = NUGGET * direction_ref[:, lanes] + own_ref[:, lanes]
        for part in range(row_ref.shape[0]):
            total = total + row_ref[part, here, :].astype(f32)
        for part in range(col_ref.shape[0]):
            total = total + col_ref[part, here, :].astype(f32)
        image_ref[:, lanes] = total
    direction, residual, image = direction_ref[...], residual_ref[...], image_ref[...]
    gram_ref[0:32, 0:32] = dot32(direction, image, NT)
    gram_ref[0:32, 32:64] = dot32(direction, residual, NT)
    gram_ref[0:32, 64:96] = dot32(residual, residual, NT)
    gram_ref[0:32, 96:128] = dot32(residual, image, NT)
    square = dot32(image, image, NT)
    for t in range(4):
        gram_ref[32:40, t * 32 : (t + 1) * 32] = square[t * 8 : (t + 1) * 8]


def solve_kernel(gram_ref, solution_ref, residual_ref, direction_ref, image_ref, solution_out, residual_out, direction_out):
    gram = gram_ref[...]
    curvature, crossing = gram[0:32, 0:32], gram[0:32, 32:64]
    norm_old, mixed = gram[0:32, 64:96], gram[0:32, 96:128]
    square = jnp.concatenate([gram[32:40, t * 32 : (t + 1) * 32] for t in range(4)], 0)
    row = lax.broadcasted_iota(jnp.int32, (32, 64), 0)
    lane = lax.broadcasted_iota(jnp.int32, (32, 64), 1)
    unit = jnp.where(row[:, :32] == lane[:, :32], 1.0, 0.0).astype(f32)
    first = jnp.concatenate([0.5 * (curvature + curvature.T), crossing], 1)
    second = jnp.concatenate([0.5 * (norm_old + norm_old.T), unit], 1)

    def eliminate(table, k):
        pivot_row = table[k : k + 1, :] / table[k : k + 1, k : k + 1]
        return jnp.where(row == k, pivot_row, table - table[:, k : k + 1] * pivot_row)

    for k in range(32):
        first, second = eliminate(first, k), eliminate(second, k)
    alpha, inverse = first[:, 32:64], second[:, 32:64]
    cross = dot32(mixed, alpha, NN)
    norm_new = 0.5 * (norm_old + norm_old.T) - cross - cross.T + dot32(alpha, dot32(square, alpha, NN), TN)
    beta = dot32(inverse, norm_new, NN)
    direction = direction_ref[...]
    residual_next = residual_ref[...] - dot32(alpha, image_ref[...], TN)
    residual_out[...] = residual_next
    solution_out[...] = solution_ref[...] + dot32(alpha, direction, TN)
    direction_out[...] = residual_next + dot32(beta, direction, TN)


def shifts(value, axis, size):
    return [lax.ppermute(value, axis, [(i, (i + k) % size) for i in range(size)]) for k in range(1, size)]


def swap(value):
    return lax.ppermute(value, "core", [(0, 1), (1, 0)])


def on_device(solution_field, residual, direction, positions, tile_pairs, pair_count):
    shape = jax.ShapeDtypeStruct
    own_points = direction.shape[1]
    y_own, core_own = lax.axis_index("y"), lax.axis_index("core")
    packed = pl.pallas_call(
        pack_kernel, out_shape=shape((288, TILE), bf16), in_specs=[VMEM] * 2, out_specs=VMEM, name="pack"
    )(direction, positions)
    chip = jnp.stack([packed, swap(packed)])
    around = shifts(chip, "y", 4)
    x_all = lax.all_gather(packed, "x")
    cols = [lax.all_gather(x_all[:, h * 144 : (h + 1) * 144], "z").reshape(32, 144, TILE) for h in range(2)]
    place = jnp.stack([pair_count[0], y_own, core_own]).astype(jnp.int32)
    bins, counts = pl.pallas_call(
        bin_kernel,
        out_shape=(shape((PARTS * BIN,), jnp.int32), shape((PARTS,), jnp.int32)),
        in_specs=[SMEM, SMEM],
        out_specs=(SMEM, SMEM),
        name="bins",
        cost_estimate=cost(8),
    )(place, tile_pairs)
    row_all = jnp.concatenate([v[:1] for v in [chip] + around] + [v[1:] for v in [chip] + around], 0)
    px, py, near, own_product = pl.pallas_call(
        row_kernel,
        out_shape=(
            shape((64, TILE, TILE), f32),
            shape((64, TILE, TILE), f32),
            shape((64, PROBES, TILE), bf16),
            shape((PROBES, own_points), f32),
        ),
        in_specs=[VMEM] * 2,
        out_specs=(VMEM,) * 4,
        compiler_params=PARAMS,
        name="rows",
        cost_estimate=cost(6),
    )(packed, row_all)
    totals = None
    col_sums = []
    for part in range(PARTS):
        last = part == PARTS - 1
        total_shape = shape((64, PROBES, TILE), f32)
        row_shape = shape((8, 256, TILE), bf16) if last else total_shape
        operands = (counts, bins, px, py, near, cols[part // 2])
        alias = {}
        scratch = [pltpu.VMEM((64, 8, TILE), f32), pltpu.VMEM((64, 8, TILE), f32), pltpu.VMEM((64, PROBES, TILE), f32)]
        if part == 1:
            totals, cols[1] = lax.optimization_barrier((totals, cols[1]))
        if part > 1:
            totals, col_sums[part - 2] = lax.optimization_barrier((totals, col_sums[part - 2]))
        if part > 0:
            operands = operands + (totals,)
            alias = {} if last else {6: 0}
        totals, col_sum = pl.pallas_call(
            functools.partial(part_kernel, part),
            out_shape=(row_shape, shape((32, 64, TILE), bf16)),
            in_specs=[SMEM] * 2 + [VMEM] * (len(operands) - 2),
            out_specs=(VMEM, VMEM),
            scratch_shapes=scratch,
            input_output_aliases=alias,
            compiler_params=PARAMS,
            name="pairs",
            cost_estimate=cost(16),
        )(*operands)
        col_sum = col_sum.reshape(8, 4 * 64, TILE)
        if part > 0:
            col_sum, col_sums[part - 1] = lax.optimization_barrier((col_sum, col_sums[part - 1]))
        col_sums.append(lax.psum_scatter(col_sum, "z", scatter_dimension=0, tiled=False).reshape(4, 64, TILE))
    row_sum = totals
    half = (row_sum[:4].astype(f32) + swap(row_sum[4:]).astype(f32)).astype(bf16)
    row_parts = [half[0]] + [
        lax.ppermute(half[k], "y", [(i, (i - k) % 4) for i in range(4)]) for k in range(1, 4)
    ]
    row_parts = jnp.stack(row_parts)
    col_parts = lax.all_to_all(jnp.concatenate(col_sums, 1), "x", 0, 0)
    image, gram = pl.pallas_call(
        gram_kernel,
        out_shape=(shape((PROBES, own_points), f32), shape((40, TILE), f32)),
        in_specs=[VMEM] * 5,
        out_specs=(VMEM, VMEM),
        compiler_params=PARAMS,
        name="gram",
    )(direction, residual, own_product, row_parts, col_parts)
    gram = gram + swap(gram)
    for axis, size in (("y", 4), ("x", 4), ("z", 8)):
        gram = sum(shifts(gram, axis, size), gram)
    return pl.pallas_call(
        solve_kernel,
        out_shape=(shape((PROBES, own_points), f32),) * 3,
        in_specs=[VMEM] * 5,
        out_specs=(VMEM,) * 3,
        compiler_params=PARAMS,
        name="solve",
    )(gram, solution_field, residual, direction, image)


def solution(mesh):
    fine = Mesh(np.asarray(mesh.devices).reshape(8, 4, 4, 2), ("z", "x", "y", "core"))
    points = P(None, ("z", "x", "y", "core"))
    return jax.shard_map(
        on_device,
        mesh=fine,
        in_specs=(points,) * 5 + (P(("z", "x", "y", "core")),),
        out_specs=(points,) * 3,
        check_vma=False,
    )
```

```python
import functools

import jax
import jax.numpy as jnp
import numpy as np
from jax import lax
from jax.experimental import pallas as pl
from jax.experimental.pallas import tpu as pltpu
from jax.sharding import Mesh
from jax.sharding import PartitionSpec as P

TILE = 128
PROBES = 32
UNROLL = 32
TAIL = 8
SPLIT = 5
BIN = 1536 + 2 * UNROLL
NUGGET = 2.0
KERNEL_SCALE = 0.1
HIGHEST = lax.Precision.HIGHEST
f32, bf16 = jnp.float32, jnp.bfloat16
VMEM = pl.BlockSpec(memory_space=pltpu.VMEM)
SMEM = pl.BlockSpec(memory_space=pltpu.SMEM)
NT = (((1,), (1,)), ((), ()))
NN = (((1,), (0,)), ((), ()))
TN = (((0,), (0,)), ((), ()))
PARAMS = pltpu.CompilerParams(vmem_limit_bytes=24 * 2**20)


def pack_kernel(direction_ref, positions_ref, packed_ref):
    for t in range(8):
        packed_ref[t * 32 : (t + 1) * 32, :] = direction_ref[:, t * TILE : (t + 1) * TILE].astype(bf16)
    where = positions_ref[...].astype(f32)
    rows = [where[d : d + 1, t * TILE : (t + 1) * TILE] for d in range(2) for t in range(8)]
    packed_ref[256:272, :] = jnp.concatenate(rows, 0).astype(bf16)


def radial(square):
    distance = pl.reciprocal(lax.rsqrt(square), approx=True)
    remain = jnp.maximum(1.0 - distance, 0.0)
    remain2 = remain * remain
    return ((remain2 * remain2) * (1.25 - remain)).astype(bf16)


def bin_kernel(place_ref, pairs_ref, bins_ref, count_ref):
    live, y_own, core_own = place_ref[0], place_ref[1], place_ref[2]

    def step(i, front):
        for u in range(8):
            e = i * 8 + u
            a, b = pairs_ref[0, e], pairs_ref[1, e]
            shift = (y_own - (a >> 4)) & 3
            slot = shift + ((((a >> 3) & 1) ^ core_own) << 2)
            entry = (slot << 3) + (a & 7) + (b << 8) + ((e < live).astype(jnp.int32) << 16)
            first = (b & 7) < SPLIT
            bins_ref[jnp.where(first, front, BIN - 1 - (e - front))] = entry
            front = front + first.astype(jnp.int32)
        return front

    groups = (live + 7) >> 3
    front = lax.fori_loop(0, groups, step, jnp.int32(0))
    back = groups * 8 - front
    count_ref[0] = front
    count_ref[1] = back
    for j in range(TAIL):
        bins_ref[front + j] = 0
        bins_ref[BIN - 1 - back - j] = SPLIT << 8


def spread(line):
    return jnp.broadcast_to(line, (TILE, TILE)).T


def part_kernel(part, *refs):
    if part == 0:
        count_ref, bins_ref, own_ref, near_ref, col_ref, row_acc, col_out, own_out, px, py, qx, qy, col_acc = refs
        row_acc[...] = jnp.zeros_like(row_acc)
        where = own_ref[256:272, :].astype(f32)
        for t in range(8):
            dx = spread(where[t : t + 1]) - where[t : t + 1]
            dy = spread(where[8 + t : 9 + t]) - where[8 + t : 9 + t]
            block = radial(dx * dx + dy * dy)
            own_out[:, t * TILE : (t + 1) * TILE] = KERNEL_SCALE * lax.dot_general(
                own_ref[t * 32 : (t + 1) * 32, :], block, NT, preferred_element_type=f32
            )
    else:
        count_ref, bins_ref, near_ref, col_ref, row_acc, row_out, col_out, px, py, qx, qy, col_acc = refs
    def row_prepare(r, carry):
        where = near_ref[r, 256:272, :].astype(f32)
        for t in range(8):
            px[r * 8 + t] = spread(where[t : t + 1])
            py[r * 8 + t] = spread(where[8 + t : 9 + t])
        return carry

    lax.fori_loop(0, 8, row_prepare, 0)
    tiles = range(SPLIT) if part == 0 else range(SPLIT, 8)
    first, number = tiles[0], len(tiles)
    live = count_ref[part]
    col_acc[...] = jnp.zeros_like(col_acc)

    def col_prepare(r, carry):
        where = col_ref[r, 256:272, :].astype(f32)
        for t in tiles:
            qx[r * 8 + t] = jnp.broadcast_to(where[t : t + 1], (8, TILE))
            qy[r * 8 + t] = jnp.broadcast_to(where[8 + t : 9 + t], (8, TILE))
        return carry

    lax.fori_loop(0, 32, col_prepare, 0)

    def several(start, size):
        results = []
        for u in range(size):
            e = start + u
            both = bins_ref[e if part == 0 else BIN - 1 - e]
            a, b = both & 63, (both >> 8) & 255
            keep = jnp.where(e < live, both >> 16, 0).astype(f32).astype(bf16)
            near = near_ref[a >> 3, pl.ds(pl.multiple_of((a & 7) * 32, 32), 32), :] * keep
            far = col_ref[b >> 3, pl.ds(pl.multiple_of((b & 7) * 32, 32), 32), :] * keep
            dx = px[a].reshape(16, 8, TILE) - qx[b][None]
            dy = py[a].reshape(16, 8, TILE) - qy[b][None]
            block = radial((dx * dx + dy * dy).reshape(TILE, TILE))
            forward = lax.dot_general(far, block, NT, preferred_element_type=f32)
            backward = lax.dot_general(near, block, NN, preferred_element_type=f32)
            results.append((a, b, forward, backward))
        for a, b, forward, backward in results:
            row_acc[a] += forward
            col_acc[b] += backward

    whole = live // UNROLL

    def body(i, carry):
        several(i * UNROLL, UNROLL)
        return carry

    def tail(i, carry):
        several(whole * UNROLL + i * TAIL, TAIL)
        return carry

    lax.fori_loop(0, whole, body, 0)
    lax.fori_loop(0, (live - whole * UNROLL + TAIL - 1) // TAIL, tail, 0)

    def finish(r, carry):
        for t in range(number):
            col_out[(r & 3) * 8 + (r >> 2), t * 32 : (t + 1) * 32, :] = (KERNEL_SCALE * col_acc[r * 8 + first + t]).astype(bf16)
        return carry

    lax.fori_loop(0, 32, finish, 0)
    if part == 1:

        def finish_row(r, carry):
            for t in range(8):
                row_out[r, t * 32 : (t + 1) * 32, :] = (KERNEL_SCALE * row_acc[r * 8 + t]).astype(bf16)
            return carry

        lax.fori_loop(0, 8, finish_row, 0)


def dot32(former, latter, dims):
    return lax.dot_general(former, latter, dims, precision=HIGHEST, preferred_element_type=f32)


def gram_kernel(direction_ref, residual_ref, own_ref, row_ref, col0_ref, col1_ref, image_ref, gram_ref):
    for t in range(8):
        here = slice(t * 32, (t + 1) * 32)
        lanes = slice(t * TILE, (t + 1) * TILE)
        total = NUGGET * direction_ref[:, lanes] + own_ref[:, lanes]
        for part in range(row_ref.shape[0]):
            total = total + row_ref[part, here, :].astype(f32)
        col_ref, place = (col0_ref, t) if t < SPLIT else (col1_ref, t - SPLIT)
        for part in range(col_ref.shape[0]):
            total = total + col_ref[part, place * 32 : (place + 1) * 32, :].astype(f32)
        image_ref[:, lanes] = total
    direction, residual, image = direction_ref[...], residual_ref[...], image_ref[...]
    gram_ref[0:32, 0:32] = dot32(direction, image, NT)
    gram_ref[0:32, 32:64] = dot32(direction, residual, NT)
    gram_ref[0:32, 64:96] = dot32(residual, residual, NT)
    gram_ref[0:32, 96:128] = dot32(residual, image, NT)
    square = dot32(image, image, NT)
    for t in range(4):
        gram_ref[32:40, t * 32 : (t + 1) * 32] = square[t * 8 : (t + 1) * 8]


def solve_kernel(gram_ref, solution_ref, residual_ref, direction_ref, image_ref, solution_out, residual_out, direction_out):
    gram = gram_ref[...]
    curvature, crossing = gram[0:32, 0:32], gram[0:32, 32:64]
    norm_old, mixed = gram[0:32, 64:96], gram[0:32, 96:128]
    square = jnp.concatenate([gram[32:40, t * 32 : (t + 1) * 32] for t in range(4)], 0)
    row = lax.broadcasted_iota(jnp.int32, (32, 64), 0)
    lane = lax.broadcasted_iota(jnp.int32, (32, 64), 1)
    unit = jnp.where(row[:, :32] == lane[:, :32], 1.0, 0.0).astype(f32)
    first = jnp.concatenate([0.5 * (curvature + curvature.T), crossing], 1)
    second = jnp.concatenate([0.5 * (norm_old + norm_old.T), unit], 1)

    def eliminate(table, k):
        pivot_row = table[k : k + 1, :] / table[k : k + 1, k : k + 1]
        return jnp.where(row == k, pivot_row, table - table[:, k : k + 1] * pivot_row)

    for k in range(32):
        first, second = eliminate(first, k), eliminate(second, k)
    alpha, inverse = first[:, 32:64], second[:, 32:64]
    cross = dot32(mixed, alpha, NN)
    norm_new = 0.5 * (norm_old + norm_old.T) - cross - cross.T + dot32(alpha, dot32(square, alpha, NN), TN)
    beta = dot32(inverse, norm_new, NN)
    direction = direction_ref[...]
    residual_next = residual_ref[...] - dot32(alpha, image_ref[...], TN)
    residual_out[...] = residual_next
    solution_out[...] = solution_ref[...] + dot32(alpha, direction, TN)
    direction_out[...] = residual_next + dot32(beta, direction, TN)


def shifts(value, axis, size):
    return [lax.ppermute(value, axis, [(i, (i + k) % size) for i in range(size)]) for k in range(1, size)]


def swap(value):
    return lax.ppermute(value, "core", [(0, 1), (1, 0)])


def on_device(solution_field, residual, direction, positions, tile_pairs, pair_count):
    shape = jax.ShapeDtypeStruct
    own_points = direction.shape[1]
    y_own, core_own = lax.axis_index("y"), lax.axis_index("core")
    packed = pl.pallas_call(
        pack_kernel, out_shape=shape((272, TILE), bf16), in_specs=[VMEM] * 2, out_specs=VMEM, name="pack"
    )(direction, positions)
    packed, other = lax.optimization_barrier((packed, swap(packed)))
    chip = jnp.stack([packed, other])
    around = shifts(chip, "y", 4)
    x_all = lax.all_gather(packed, "x")
    x_all, around = lax.optimization_barrier((x_all, around))
    col_all = lax.all_gather(x_all, "z").reshape(32, 272, TILE)
    row_all = jnp.concatenate([v[:1] for v in [chip] + around] + [v[1:] for v in [chip] + around], 0)
    place = jnp.stack([pair_count[0], y_own, core_own]).astype(jnp.int32)
    bins, counts = pl.pallas_call(
        bin_kernel,
        out_shape=(shape((BIN,), jnp.int32), shape((2,), jnp.int32)),
        in_specs=[SMEM, SMEM],
        out_specs=(SMEM, SMEM),
        name="bins",
    )(place, tile_pairs)
    acc = shape((64, PROBES, TILE), f32)
    scratch = [pltpu.VMEM((64, TILE, TILE), f32)] * 2
    scratch += [pltpu.VMEM((256, 8, TILE), f32), pltpu.VMEM((256, 8, TILE), f32), pltpu.VMEM((256, PROBES, TILE), f32)]

    def reduced(col_out):
        number = col_out.shape[1] // 32
        blocks = lax.all_to_all(col_out.reshape(4, 8 * number * 32, TILE), "x", 0, 0)
        blocks = jnp.sum(blocks.astype(f32), 0).astype(bf16)
        return blocks.reshape(8, number * 32, TILE)

    row_acc, col_first, own_product = pl.pallas_call(
        functools.partial(part_kernel, 0),
        out_shape=(acc, shape((32, SPLIT * 32, TILE), bf16), shape((PROBES, own_points), f32)),
        in_specs=[SMEM] * 2 + [VMEM] * 3,
        out_specs=(VMEM,) * 3,
        scratch_shapes=scratch,
        compiler_params=PARAMS,
        name="pairs_first",
    )(counts, bins, packed, row_all, col_all)
    row_sum, col_second = pl.pallas_call(
        functools.partial(part_kernel, 1),
        out_shape=(shape((8, 256, TILE), bf16), shape((32, (8 - SPLIT) * 32, TILE), bf16)),
        in_specs=[SMEM] * 2 + [VMEM] * 3,
        out_specs=(VMEM,) * 2,
        scratch_shapes=scratch,
        compiler_params=PARAMS,
        name="pairs_second",
    )(counts, bins, row_all, col_all, row_acc)
    first = reduced(col_first)
    second, first = lax.optimization_barrier((col_second, first))
    second = reduced(second)
    col_first = lax.all_to_all(first, "z", 0, 0)
    half = (row_sum[:4].astype(f32) + swap(row_sum[4:]).astype(f32)).astype(bf16)
    row_parts = [half[0]] + [
        lax.ppermute(half[k], "y", [(i, (i - k) % 4) for i in range(4)]) for k in range(1, 4)
    ]
    row_parts = jnp.stack(row_parts)
    col_second = lax.all_to_all(second, "z", 0, 0)
    image, gram = pl.pallas_call(
        gram_kernel,
        out_shape=(shape((PROBES, own_points), f32), shape((40, TILE), f32)),
        in_specs=[VMEM] * 6,
        out_specs=(VMEM, VMEM),
        compiler_params=PARAMS,
        name="gram",
    )(direction, residual, own_product, row_parts, col_first, col_second)
    gram = gram + swap(gram)
    for axis, size in (("y", 4), ("x", 4), ("z", 8)):
        gram = sum(shifts(gram, axis, size), gram)
    return pl.pallas_call(
        solve_kernel,
        out_shape=(shape((PROBES, own_points), f32),) * 3,
        in_specs=[VMEM] * 5,
        out_specs=(VMEM,) * 3,
        compiler_params=PARAMS,
        name="solve",
    )(gram, solution_field, residual, direction, image)


def solution(mesh):
    fine = Mesh(np.asarray(mesh.devices).reshape(8, 4, 4, 2), ("z", "x", "y", "core"))
    points = P(None, ("z", "x", "y", "core"))
    return jax.shard_map(
        on_device,
        mesh=fine,
        in_specs=(points,) * 5 + (P(("z", "x", "y", "core")),),
        out_specs=(points,) * 3,
        check_vma=False,
    )
```

```python
import functools

import jax
import jax.numpy as jnp
import numpy as np
from jax import lax
from jax.experimental import pallas as pl
from jax.experimental.pallas import tpu as pltpu
from jax.sharding import Mesh
from jax.sharding import PartitionSpec as P

TILE = 128
PROBES = 32
UNROLL = 32
TAIL = 8
SPLIT = 6
BIN = 1536 + 2 * UNROLL
NUGGET = 2.0
KERNEL_SCALE = 0.1
HIGHEST = lax.Precision.HIGHEST
f32, bf16 = jnp.float32, jnp.bfloat16
VMEM = pl.BlockSpec(memory_space=pltpu.VMEM)
SMEM = pl.BlockSpec(memory_space=pltpu.SMEM)
NT = (((1,), (1,)), ((), ()))
NN = (((1,), (0,)), ((), ()))
TN = (((0,), (0,)), ((), ()))
PARAMS = pltpu.CompilerParams(vmem_limit_bytes=24 * 2**20)


def pack_kernel(direction_ref, positions_ref, packed_ref):
    for t in range(8):
        packed_ref[t * 32 : (t + 1) * 32, :] = direction_ref[:, t * TILE : (t + 1) * TILE].astype(bf16)
    where = positions_ref[...].astype(f32)
    rows = [where[d : d + 1, t * TILE : (t + 1) * TILE] for d in range(2) for t in range(8)]
    packed_ref[256:272, :] = jnp.concatenate(rows, 0).astype(bf16)


def radial(square):
    distance = pl.reciprocal(lax.rsqrt(square), approx=True)
    remain = jnp.maximum(1.0 - distance, 0.0)
    remain2 = remain * remain
    return ((remain2 * remain2) * (1.25 - remain)).astype(bf16)


def bin_kernel(place_ref, pairs_ref, after_ref, bins_ref, count_ref):
    live, x_own, y_own, core_own = place_ref[0], place_ref[1], place_ref[2], place_ref[3]

    def step(i, front):
        for u in range(8):
            e = i * 8 + u
            a, b = pairs_ref[0, e], pairs_ref[1, e]
            shift = (y_own - (a >> 4)) & 3
            slot = shift + ((((a >> 3) & 1) ^ core_own) << 2)
            far = ((((x_own - (b >> 3)) & 3) << 3) + (b >> 5) << 3) + (b & 7)
            entry = (slot << 3) + (a & 7) + (far << 8) + ((e < live).astype(jnp.int32) << 16)
            first = (b & 7) < SPLIT
            bins_ref[jnp.where(first, front, BIN - 1 - (e - front))] = entry
            front = front + first.astype(jnp.int32)
        return front

    groups = (live + 7) >> 3
    front = lax.fori_loop(0, groups, step, jnp.int32(0))
    back = groups * 8 - front
    count_ref[0] = front
    count_ref[1] = back
    for j in range(TAIL):
        bins_ref[front + j] = 0
        bins_ref[BIN - 1 - back - j] = SPLIT << 8


def spread(strip, t):
    return jnp.broadcast_to(strip[:, t : t + 1], (TILE, TILE))


def part_kernel(part, *refs):
    if part == 0:
        count_ref, bins_ref, own_ref, near_ref, col_ref, row_acc, own_out, *col_out, px, py, qx, qy, col_acc = refs
        row_acc[...] = jnp.zeros_like(row_acc)
        where = own_ref[256:272, :].astype(f32)
        strip = where.T
        for t in range(8):
            dx = spread(strip, t) - where[t : t + 1]
            dy = spread(strip, 8 + t) - where[8 + t : 9 + t]
            block = radial(dx * dx + dy * dy)
            own_out[:, t * TILE : (t + 1) * TILE] = KERNEL_SCALE * lax.dot_general(
                own_ref[t * 32 : (t + 1) * 32, :], block, NT, preferred_element_type=f32
            )
    else:
        count_ref, bins_ref, near_ref, col_ref, row_acc, row_out, *col_out, px, py, qx, qy, col_acc = refs
    def row_prepare(r, carry):
        strip = near_ref[r, 256:272, :].astype(f32).T
        for t in range(8):
            px[r * 8 + t] = spread(strip, t)
            py[r * 8 + t] = spread(strip, 8 + t)
        return carry

    lax.fori_loop(0, 8, row_prepare, 0)
    tiles = range(SPLIT) if part == 0 else range(SPLIT, 8)
    first, number = tiles[0], len(tiles)
    live = count_ref[part]
    col_acc[...] = jnp.zeros_like(col_acc)

    def col_prepare(r, carry):
        where = col_ref[(r & 7) * 4 + (r >> 3), 256:272, :].astype(f32)
        for t in tiles:
            qx[r * 8 + t] = jnp.broadcast_to(where[t : t + 1], (8, TILE))
            qy[r * 8 + t] = jnp.broadcast_to(where[8 + t : 9 + t], (8, TILE))
        return carry

    lax.fori_loop(0, 32, col_prepare, 0)

    def several(start, size):
        results = []
        for u in range(size):
            e = start + u
            both = bins_ref[e if part == 0 else BIN - 1 - e]
            a, b = both & 63, (both >> 8) & 255
            keep = jnp.where(e < live, both >> 16, 0).astype(f32).astype(bf16)
            near = near_ref[a >> 3, pl.ds(pl.multiple_of((a & 7) * 32, 32), 32), :] * keep
            far = col_ref[((b >> 3) & 7) * 4 + (b >> 6), pl.ds(pl.multiple_of((b & 7) * 32, 32), 32), :] * keep
            dx = px[a].reshape(16, 8, TILE) - qx[b][None]
            dy = py[a].reshape(16, 8, TILE) - qy[b][None]
            block = radial((dx * dx + dy * dy).reshape(TILE, TILE))
            forward = lax.dot_general(far, block, NT, preferred_element_type=f32)
            backward = lax.dot_general(near, block, NN, preferred_element_type=f32)
            results.append((a, b, forward, backward))
        for a, b, forward, backward in results:
            row_acc[a] += forward
            col_acc[b] += backward

    whole = live // UNROLL

    def body(i, carry):
        several(i * UNROLL, UNROLL)
        return carry

    def tail(i, carry):
        several(whole * UNROLL + i * TAIL, TAIL)
        return carry

    lax.fori_loop(0, whole, body, 0)
    lax.fori_loop(0, (live - whole * UNROLL + TAIL - 1) // TAIL, tail, 0)

    def finish(z, carry):
        for k in range(4):
            for t in range(number):
                total = KERNEL_SCALE * col_acc[k * 64 + z * 8 + first + t]
                col_out[k][z, t * 32 : (t + 1) * 32, :] = total.astype(bf16)
        return carry

    lax.fori_loop(0, 8, finish, 0)
    if part == 1:

        def finish_row(r, carry):
            for t in range(8):
                row_out[r, t * 32 : (t + 1) * 32, :] = (KERNEL_SCALE * row_acc[r * 8 + t]).astype(bf16)
            return carry

        lax.fori_loop(0, 8, finish_row, 0)


def add_kernel(own0, a0, b0, c0, own1, a1, b1, c1, out):
    for z in range(8):
        for rows, parts in ((slice(0, SPLIT * 32), (own0, a0, b0, c0)), (slice(SPLIT * 32, 256), (own1, a1, b1, c1))):
            total = parts[0][z].astype(f32)
            for part in parts[1:]:
                total = total + part[z].astype(f32)
            out[z, rows, :] = total.astype(bf16)


def dot32(former, latter, dims):
    return lax.dot_general(former, latter, dims, precision=HIGHEST, preferred_element_type=f32)


def gram_kernel(direction_ref, residual_ref, own_ref, row_ref, col_ref, image_ref, gram_ref):
    for t in range(8):
        here = slice(t * 32, (t + 1) * 32)
        lanes = slice(t * TILE, (t + 1) * TILE)
        total = NUGGET * direction_ref[:, lanes] + own_ref[:, lanes]
        for part in range(row_ref.shape[0]):
            total = total + row_ref[part, here, :].astype(f32)
        for part in range(col_ref.shape[0]):
            total = total + col_ref[part, here, :].astype(f32)
        image_ref[:, lanes] = total
    direction, residual, image = direction_ref[...], residual_ref[...], image_ref[...]
    gram_ref[0:32, 0:32] = dot32(direction, image, NT)
    gram_ref[0:32, 32:64] = dot32(direction, residual, NT)
    gram_ref[0:32, 64:96] = dot32(residual, residual, NT)
    gram_ref[0:32, 96:128] = dot32(residual, image, NT)
    square = dot32(image, image, NT)
    for t in range(4):
        gram_ref[32:40, t * 32 : (t + 1) * 32] = square[t * 8 : (t + 1) * 8]


def solve_kernel(gram_ref, solution_ref, residual_ref, direction_ref, image_ref, solution_out, residual_out, direction_out):
    gram = gram_ref[...]
    curvature, crossing = gram[0:32, 0:32], gram[0:32, 32:64]
    norm_old, mixed = gram[0:32, 64:96], gram[0:32, 96:128]
    square = jnp.concatenate([gram[32:40, t * 32 : (t + 1) * 32] for t in range(4)], 0)
    row = lax.broadcasted_iota(jnp.int32, (32, 64), 0)
    lane = lax.broadcasted_iota(jnp.int32, (32, 64), 1)
    unit = jnp.where(row[:, :32] == lane[:, :32], 1.0, 0.0).astype(f32)
    first = jnp.concatenate([0.5 * (curvature + curvature.T), crossing], 1)
    second = jnp.concatenate([0.5 * (norm_old + norm_old.T), unit], 1)

    def eliminate(table, k):
        pivot_row = table[k : k + 1, :] / table[k : k + 1, k : k + 1]
        return jnp.where(row == k, pivot_row, table - table[:, k : k + 1] * pivot_row)

    for k in range(32):
        first, second = eliminate(first, k), eliminate(second, k)
    alpha, inverse = first[:, 32:64], second[:, 32:64]
    cross = dot32(mixed, alpha, NN)
    norm_new = 0.5 * (norm_old + norm_old.T) - cross - cross.T + dot32(alpha, dot32(square, alpha, NN), TN)
    beta = dot32(inverse, norm_new, NN)
    direction = direction_ref[...]
    residual_next = residual_ref[...] - dot32(alpha, image_ref[...], TN)
    residual_out[...] = residual_next
    solution_out[...] = solution_ref[...] + dot32(alpha, direction, TN)
    direction_out[...] = residual_next + dot32(beta, direction, TN)


def shifts(value, axis, size):
    return [lax.ppermute(value, axis, [(i, (i + k) % size) for i in range(size)]) for k in range(1, size)]


def swap(value):
    return lax.ppermute(value, "core", [(0, 1), (1, 0)])


def on_device(solution_field, residual, direction, positions, tile_pairs, pair_count):
    shape = jax.ShapeDtypeStruct
    own_points = direction.shape[1]
    x_own, y_own, core_own = lax.axis_index("x"), lax.axis_index("y"), lax.axis_index("core")
    packed = pl.pallas_call(
        pack_kernel, out_shape=shape((272, TILE), bf16), in_specs=[VMEM] * 2, out_specs=VMEM, name="pack"
    )(direction, positions)
    x_all = jnp.stack([packed] + shifts(packed, "x", 4))
    col_all = lax.all_gather(x_all, "z").reshape(32, 272, TILE)
    chip = jnp.stack([packed, swap(packed)])
    around = shifts(chip, "y", 4)
    row_all = jnp.concatenate([v[:1] for v in [chip] + around] + [v[1:] for v in [chip] + around], 0)
    place = jnp.stack([pair_count[0], x_own, y_own, core_own]).astype(jnp.int32)
    bins, counts = pl.pallas_call(
        bin_kernel,
        out_shape=(shape((BIN,), jnp.int32), shape((2,), jnp.int32)),
        in_specs=[SMEM, SMEM, pl.BlockSpec(memory_space=pl.ANY)],
        out_specs=(SMEM, SMEM),
        name="bins",
    )(place, tile_pairs, row_all)
    acc = shape((64, PROBES, TILE), f32)
    scratch = [pltpu.VMEM((64, TILE, TILE), f32)] * 2
    scratch += [pltpu.VMEM((256, 8, TILE), f32), pltpu.VMEM((256, 8, TILE), f32), pltpu.VMEM((256, PROBES, TILE), f32)]

    def blocks(number):
        return (shape((8, number * 32, TILE), bf16),) * 4

    def sent(col_out):
        return [lax.ppermute(col_out[k], "x", [(i, (i - k) % 4) for i in range(4)]) for k in range(1, 4)]

    row_acc, own_product, *col_first = pl.pallas_call(
        functools.partial(part_kernel, 0),
        out_shape=(acc, shape((PROBES, own_points), f32)) + blocks(SPLIT),
        in_specs=[SMEM] * 2 + [VMEM] * 3,
        out_specs=(VMEM,) * 6,
        scratch_shapes=scratch,
        compiler_params=PARAMS,
        name="pairs_first",
    )(counts, bins, packed, row_all, col_all)
    row_sum, *col_second = pl.pallas_call(
        functools.partial(part_kernel, 1),
        out_shape=(shape((8, 256, TILE), bf16),) + blocks(8 - SPLIT),
        in_specs=[SMEM] * 2 + [VMEM] * 3,
        out_specs=(VMEM,) * 5,
        scratch_shapes=scratch,
        compiler_params=PARAMS,
        name="pairs_second",
    )(counts, bins, row_all, col_all, row_acc)
    sums = pl.pallas_call(
        add_kernel,
        out_shape=shape((8, 256, TILE), bf16),
        in_specs=[VMEM] * 8,
        out_specs=VMEM,
        compiler_params=PARAMS,
        name="add",
    )(col_first[0], *sent(col_first), col_second[0], *sent(col_second))
    col_parts = lax.all_to_all(sums, "z", 0, 0)
    half = (row_sum[:4].astype(f32) + swap(row_sum[4:]).astype(f32)).astype(bf16)
    row_parts = [half[0]] + [
        lax.ppermute(half[k], "y", [(i, (i - k) % 4) for i in range(4)]) for k in range(1, 4)
    ]
    row_parts = jnp.stack(row_parts)
    image, gram = pl.pallas_call(
        gram_kernel,
        out_shape=(shape((PROBES, own_points), f32), shape((40, TILE), f32)),
        in_specs=[VMEM] * 5,
        out_specs=(VMEM, VMEM),
        compiler_params=PARAMS,
        name="gram",
    )(direction, residual, own_product, row_parts, col_parts)
    gram = gram + swap(gram)
    gram = sum(shifts(gram, "y", 4), gram)
    gram = sum(shifts(gram, "x", 4), gram)
    gram = gram + lax.ppermute(gram, "z", [(i, (i + 4) % 8) for i in range(8)])
    gram = sum(shifts(gram, "z", 8)[:3], gram)
    return pl.pallas_call(
        solve_kernel,
        out_shape=(shape((PROBES, own_points), f32),) * 3,
        in_specs=[VMEM] * 5,
        out_specs=(VMEM,) * 3,
        compiler_params=PARAMS,
        name="solve",
    )(gram, solution_field, residual, direction, image)


def solution(mesh):
    fine = Mesh(np.asarray(mesh.devices).reshape(8, 4, 4, 2), ("z", "x", "y", "core"))
    points = P(None, ("z", "x", "y", "core"))
    return jax.shard_map(
        on_device,
        mesh=fine,
        in_specs=(points,) * 5 + (P(("z", "x", "y", "core")),),
        out_specs=(points,) * 3,
        check_vma=False,
    )
```

```python
import functools

import jax
import jax.numpy as jnp
import numpy as np
from jax import lax
from jax.experimental import pallas as pl
from jax.experimental.pallas import tpu as pltpu
from jax.sharding import Mesh
from jax.sharding import PartitionSpec as P

TILE = 128
PROBES = 32
UNROLL = 32
TAIL = 8
SPLIT = 6
BIN = 1536 + 2 * UNROLL
NUGGET = 2.0
KERNEL_SCALE = 0.1
HIGHEST = lax.Precision.HIGHEST
f32, bf16 = jnp.float32, jnp.bfloat16
VMEM = pl.BlockSpec(memory_space=pltpu.VMEM)
SMEM = pl.BlockSpec(memory_space=pltpu.SMEM)
NT = (((1,), (1,)), ((), ()))
NN = (((1,), (0,)), ((), ()))
TN = (((0,), (0,)), ((), ()))
PARAMS = pltpu.CompilerParams(vmem_limit_bytes=16 * 2**20)
SMALL = pltpu.CompilerParams(vmem_limit_bytes=4 * 2**20)


def pack_kernel(direction_ref, positions_ref, packed_ref):
    for t in range(8):
        packed_ref[t * 32 : (t + 1) * 32, :] = direction_ref[:, t * TILE : (t + 1) * TILE].astype(bf16)
    where = positions_ref[...].astype(f32)
    rows = [where[d : d + 1, t * TILE : (t + 1) * TILE] for d in range(2) for t in range(8)]
    packed_ref[256:272, :] = jnp.concatenate(rows, 0).astype(bf16)


def radial(square):
    distance = pl.reciprocal(lax.rsqrt(square), approx=True)
    remain = jnp.maximum(1.0 - distance, 0.0)
    remain2 = remain * remain
    return ((remain2 * remain2) * (1.25 - remain)).astype(bf16)


def bin_kernel(live_ref, pairs_ref, after_ref, bins_ref, count_ref):
    live = live_ref[0]

    def put(e, front):
        a, b = pairs_ref[0, e], pairs_ref[1, e]
        first = (b & 7) < SPLIT
        bins_ref[jnp.where(first, front, BIN - 1 - e + front)] = a + (b << 8)
        return front + first.astype(jnp.int32)

    def step(i, front):
        for u in range(8):
            front = put(i * 8 + u, front)
        return front

    groups = live >> 3
    front = lax.fori_loop(0, groups, step, jnp.int32(0))
    front = lax.fori_loop(groups * 8, live, put, front)
    back = live - front
    count_ref[0] = front
    count_ref[1] = back
    for j in range(TAIL):
        bins_ref[front + j] = 0
        bins_ref[BIN - 1 - back - j] = SPLIT << 8


def spread(strip, t):
    return jnp.broadcast_to(strip[:, t : t + 1], (TILE, TILE))


def row_kernel(own_ref, near_ref, px, py, own_out):
    def row_prepare(r, carry):
        strip = near_ref[r, 256:272, :].astype(f32).T
        for t in range(8):
            px[r * 8 + t] = spread(strip, t)
            py[r * 8 + t] = spread(strip, 8 + t)
        return carry

    lax.fori_loop(0, 8, row_prepare, 0)
    where = own_ref[256:272, :].astype(f32)
    strip = where.T
    for t in range(8):
        dx = spread(strip, t) - where[t : t + 1]
        dy = spread(strip, 8 + t) - where[8 + t : 9 + t]
        block = radial(dx * dx + dy * dy)
        own_out[:, t * TILE : (t + 1) * TILE] = KERNEL_SCALE * lax.dot_general(
            own_ref[t * 32 : (t + 1) * 32, :], block, NT, preferred_element_type=f32
        )


def part_kernel(part, place_ref, count_ref, bins_ref, near_ref, px, py, col_ref, *refs):
    if part == 0:
        row_acc, *col_out, qx, qy, col_acc = refs
        row_acc[...] = jnp.zeros_like(row_acc)
    else:
        row_acc, row_out, *col_out, qx, qy, col_acc = refs
    x_own, y_own, z_own, core_own = place_ref[0], place_ref[1], place_ref[2], place_ref[3]
    tiles = range(SPLIT) if part == 0 else range(SPLIT, 8)
    first, number = tiles[0], len(tiles)
    live = count_ref[part]
    col_acc[...] = jnp.zeros_like(col_acc)

    def col_prepare(r, carry):
        where = col_ref[r, 256:272, :].astype(f32)
        for t in tiles:
            qx[r * 8 + t] = jnp.broadcast_to(where[t : t + 1], (8, TILE))
            qy[r * 8 + t] = jnp.broadcast_to(where[8 + t : 9 + t], (8, TILE))
        return carry

    lax.fori_loop(0, 32, col_prepare, 0)

    def several(start, size):
        results = []
        for u in range(size):
            e = start + u
            both = bins_ref[e if part == 0 else BIN - 1 - e]
            a, b = both & 255, both >> 8
            keep = jnp.where(e < live, 1.0, 0.0).astype(bf16)
            near_slot = ((y_own - (a >> 4)) & 3) + ((((a >> 3) & 1) ^ core_own) << 2)
            far_slot = (((x_own - (b >> 3)) & 3) << 3) + ((z_own - (b >> 5)) & 7)
            near = near_ref[near_slot, pl.ds(pl.multiple_of((a & 7) * 32, 32), 32), :] * keep
            far = col_ref[far_slot, pl.ds(pl.multiple_of((b & 7) * 32, 32), 32), :] * keep
            a = (near_slot << 3) + (a & 7)
            b = (far_slot << 3) + (b & 7)
            dx = px[a].reshape(16, 8, TILE) - qx[b][None]
            dy = py[a].reshape(16, 8, TILE) - qy[b][None]
            block = radial((dx * dx + dy * dy).reshape(TILE, TILE))
            forward = lax.dot_general(far, block, NT, preferred_element_type=f32)
            backward = lax.dot_general(near, block, NN, preferred_element_type=f32)
            results.append((a, b, forward, backward))
        for a, b, forward, backward in results:
            row_acc[a] += forward
            col_acc[b] += backward

    whole = live // UNROLL

    def body(i, carry):
        several(i * UNROLL, UNROLL)
        return carry

    def tail(i, carry):
        several(whole * UNROLL + i * TAIL, TAIL)
        return carry

    lax.fori_loop(0, whole, body, 0)
    lax.fori_loop(0, (live - whole * UNROLL + TAIL - 1) // TAIL, tail, 0)

    def finish(z, carry):
        for k in range(4):
            for t in range(number):
                total = KERNEL_SCALE * col_acc[k * 64 + z * 8 + first + t]
                col_out[k][(z_own - z) & 7, t * 32 : (t + 1) * 32, :] = total.astype(bf16)
        return carry

    lax.fori_loop(0, 8, finish, 0)
    if part == 1:

        def finish_row(r, carry):
            for t in range(8):
                row_out[r, t * 32 : (t + 1) * 32, :] = (KERNEL_SCALE * row_acc[r * 8 + t]).astype(bf16)
            return carry

        lax.fori_loop(0, 8, finish_row, 0)


def add_kernel(own0, a0, b0, c0, own1, a1, b1, c1, out):
    for z in range(8):
        for rows, parts in ((slice(0, SPLIT * 32), (own0, a0, b0, c0)), (slice(SPLIT * 32, 256), (own1, a1, b1, c1))):
            total = parts[0][z].astype(f32)
            for part in parts[1:]:
                total = total + part[z].astype(f32)
            out[z, rows, :] = total.astype(bf16)


def dot32(former, latter, dims):
    return lax.dot_general(former, latter, dims, precision=HIGHEST, preferred_element_type=f32)


def gram_kernel(direction_ref, residual_ref, own_ref, row_ref, col_ref, image_ref, gram_ref):
    for t in range(8):
        here = slice(t * 32, (t + 1) * 32)
        lanes = slice(t * TILE, (t + 1) * TILE)
        total = NUGGET * direction_ref[:, lanes] + own_ref[:, lanes]
        for part in range(row_ref.shape[0]):
            total = total + row_ref[part, here, :].astype(f32)
        for part in range(col_ref.shape[0]):
            total = total + col_ref[part, here, :].astype(f32)
        image_ref[:, lanes] = total
    direction, residual, image = direction_ref[...], residual_ref[...], image_ref[...]
    gram_ref[0:32, 0:32] = dot32(direction, image, NT)
    gram_ref[0:32, 32:64] = dot32(direction, residual, NT)
    gram_ref[0:32, 64:96] = dot32(residual, residual, NT)
    gram_ref[0:32, 96:128] = dot32(residual, image, NT)
    square = dot32(image, image, NT)
    for t in range(4):
        gram_ref[32:40, t * 32 : (t + 1) * 32] = square[t * 8 : (t + 1) * 8]


def solve_kernel(gram_ref, solution_ref, residual_ref, direction_ref, image_ref, solution_out, residual_out, direction_out):
    gram = gram_ref[...]
    curvature, crossing = gram[0:32, 0:32], gram[0:32, 32:64]
    norm_old, mixed = gram[0:32, 64:96], gram[0:32, 96:128]
    square = jnp.concatenate([gram[32:40, t * 32 : (t + 1) * 32] for t in range(4)], 0)
    row = lax.broadcasted_iota(jnp.int32, (32, 64), 0)
    lane = lax.broadcasted_iota(jnp.int32, (32, 64), 1)
    unit = jnp.where(row[:, :32] == lane[:, :32], 1.0, 0.0).astype(f32)
    first = jnp.concatenate([0.5 * (curvature + curvature.T), crossing], 1)
    second = jnp.concatenate([0.5 * (norm_old + norm_old.T), unit], 1)

    def eliminate(table, k):
        pivot_row = table[k : k + 1, :] / table[k : k + 1, k : k + 1]
        return jnp.where(row == k, pivot_row, table - table[:, k : k + 1] * pivot_row)

    for k in range(32):
        first, second = eliminate(first, k), eliminate(second, k)
    alpha, inverse = first[:, 32:64], second[:, 32:64]
    cross = dot32(mixed, alpha, NN)
    norm_new = 0.5 * (norm_old + norm_old.T) - cross - cross.T + dot32(alpha, dot32(square, alpha, NN), TN)
    beta = dot32(inverse, norm_new, NN)
    direction = direction_ref[...]
    residual_next = residual_ref[...] - dot32(alpha, image_ref[...], TN)
    residual_out[...] = residual_next
    solution_out[...] = solution_ref[...] + dot32(alpha, direction, TN)
    direction_out[...] = residual_next + dot32(beta, direction, TN)


def shifts(value, axis, size):
    return [lax.ppermute(value, axis, [(i, (i + k) % size) for i in range(size)]) for k in range(1, size)]


def swap(value):
    return lax.ppermute(value, "core", [(0, 1), (1, 0)])


def on_device(solution_field, residual, direction, positions, tile_pairs, pair_count):
    shape = jax.ShapeDtypeStruct
    own_points = direction.shape[1]
    packed = pl.pallas_call(
        pack_kernel, out_shape=shape((272, TILE), bf16), in_specs=[VMEM] * 2, out_specs=VMEM, compiler_params=SMALL, name="pack"
    )(direction, positions)
    z_all = jnp.stack([packed] + shifts(packed, "z", 8))
    up, down = [(i, (i + 1) % 4) for i in range(4)], [(i, (i - 1) % 4) for i in range(4)]
    x_below, x_above = lax.ppermute(z_all, "x", up), lax.ppermute(z_all, "x", down)
    x_far = [lax.ppermute(x_below[:4], "x", up), lax.ppermute(x_above[4:], "x", down)]
    col_all = jnp.concatenate([z_all, x_below, *x_far, x_above], 0)
    chip = jnp.stack([packed, swap(packed)])
    around = shifts(chip, "y", 4)
    row_all = jnp.concatenate([v[:1] for v in [chip] + around] + [v[1:] for v in [chip] + around], 0)
    place = jnp.stack([lax.axis_index(name) for name in ("x", "y", "z", "core")]).astype(jnp.int32)
    bins, counts = pl.pallas_call(
        bin_kernel,
        out_shape=(shape((BIN,), jnp.int32), shape((2,), jnp.int32)),
        in_specs=[SMEM, SMEM, VMEM],
        out_specs=(SMEM, SMEM),
        compiler_params=SMALL,
        name="bins",
    )(pair_count, tile_pairs, x_above[0, :16])
    spread_shape = shape((64, TILE, TILE), f32)
    px, py, own_product = pl.pallas_call(
        row_kernel,
        out_shape=(spread_shape, spread_shape, shape((PROBES, own_points), f32)),
        in_specs=[VMEM] * 2,
        out_specs=(VMEM,) * 3,
        compiler_params=PARAMS,
        name="rows",
    )(packed, row_all)
    acc = shape((64, PROBES, TILE), f32)
    scratch = [pltpu.VMEM((256, 8, TILE), f32), pltpu.VMEM((256, 8, TILE), f32), pltpu.VMEM((256, PROBES, TILE), f32)]

    def blocks(number):
        return (shape((8, number * 32, TILE), bf16),) * 4

    def sent(col_out):
        return [lax.ppermute(col_out[k], "x", [(i, (i - k) % 4) for i in range(4)]) for k in range(1, 4)]

    row_acc, *col_first = pl.pallas_call(
        functools.partial(part_kernel, 0),
        out_shape=(acc,) + blocks(SPLIT),
        in_specs=[SMEM] * 3 + [VMEM] * 4,
        out_specs=(VMEM,) * 5,
        scratch_shapes=scratch,
        compiler_params=PARAMS,
        name="pairs_first",
    )(place, counts, bins, row_all, px, py, col_all)
    row_sum, *col_second = pl.pallas_call(
        functools.partial(part_kernel, 1),
        out_shape=(shape((8, 256, TILE), bf16),) + blocks(8 - SPLIT),
        in_specs=[SMEM] * 3 + [VMEM] * 5,
        out_specs=(VMEM,) * 5,
        scratch_shapes=scratch,
        compiler_params=PARAMS,
        name="pairs_second",
    )(place, counts, bins, row_all, px, py, col_all, row_acc)
    sums = pl.pallas_call(
        add_kernel,
        out_shape=shape((8, 256, TILE), bf16),
        in_specs=[VMEM] * 8,
        out_specs=VMEM,
        compiler_params=PARAMS,
        name="add",
    )(col_first[0], *sent(col_first), col_second[0], *sent(col_second))
    col_parts = lax.all_to_all(sums, "z", 0, 0)
    half = (row_sum[:4].astype(f32) + swap(row_sum[4:]).astype(f32)).astype(bf16)
    row_parts = [half[0]] + [
        lax.ppermute(half[k], "y", [(i, (i - k) % 4) for i in range(4)]) for k in range(1, 4)
    ]
    row_parts = jnp.stack(row_parts)
    image, gram = pl.pallas_call(
        gram_kernel,
        out_shape=(shape((PROBES, own_points), f32), shape((40, TILE), f32)),
        in_specs=[VMEM] * 5,
        out_specs=(VMEM, VMEM),
        compiler_params=PARAMS,
        name="gram",
    )(direction, residual, own_product, row_parts, col_parts)
    gram = gram + swap(gram)
    gram = sum(shifts(gram, "y", 4), gram)
    gram = sum(shifts(gram, "x", 4), gram)
    gram = gram + lax.ppermute(gram, "z", [(i, (i + 4) % 8) for i in range(8)])
    gram = sum(shifts(gram, "z", 8)[:3], gram)
    return pl.pallas_call(
        solve_kernel,
        out_shape=(shape((PROBES, own_points), f32),) * 3,
        in_specs=[VMEM] * 5,
        out_specs=(VMEM,) * 3,
        compiler_params=PARAMS,
        name="solve",
    )(gram, solution_field, residual, direction, image)


def solution(mesh):
    fine = Mesh(np.asarray(mesh.devices).reshape(8, 4, 4, 2), ("z", "x", "y", "core"))
    points = P(None, ("z", "x", "y", "core"))
    return jax.shard_map(
        on_device,
        mesh=fine,
        in_specs=(points,) * 5 + (P(("z", "x", "y", "core")),),
        out_specs=(points,) * 3,
        check_vma=False,
    )
```

```python
import functools

import jax
import jax.numpy as jnp
import numpy as np
from jax import lax
from jax.experimental import pallas as pl
from jax.experimental.pallas import tpu as pltpu
from jax.sharding import Mesh
from jax.sharding import PartitionSpec as P

TILE = 128
PROBES = 32
UNROLL = 32
TAIL = 8
SPLIT = 6
BIN = 1536 + 2 * UNROLL
NUGGET = 2.0
KERNEL_SCALE = 0.1
HIGHEST = lax.Precision.HIGHEST
f32, bf16 = jnp.float32, jnp.bfloat16
VMEM = pl.BlockSpec(memory_space=pltpu.VMEM)
SMEM = pl.BlockSpec(memory_space=pltpu.SMEM)
NT = (((1,), (1,)), ((), ()))
NN = (((1,), (0,)), ((), ()))
TN = (((0,), (0,)), ((), ()))
PARAMS = pltpu.CompilerParams(vmem_limit_bytes=16 * 2**20)
SMALL = pltpu.CompilerParams(vmem_limit_bytes=4 * 2**20)


def pack_kernel(direction_ref, positions_ref, packed_ref):
    for t in range(8):
        packed_ref[t * 32 : (t + 1) * 32, :] = direction_ref[:, t * TILE : (t + 1) * TILE].astype(bf16)
    where = positions_ref[...].astype(f32)
    rows = [where[d : d + 1, t * TILE : (t + 1) * TILE] for d in range(2) for t in range(8)]
    packed_ref[256:272, :] = jnp.concatenate(rows, 0).astype(bf16)


def radial(square):
    distance = pl.reciprocal(lax.rsqrt(square), approx=True)
    remain = jnp.maximum(1.0 - distance, 0.0)
    remain2 = remain * remain
    return ((remain2 * remain2) * (1.25 - remain)).astype(bf16)


def bin_kernel(live_ref, pairs_ref, after_ref, bins_ref, count_ref):
    live = live_ref[0]

    def put(e, front):
        a, b = pairs_ref[0, e], pairs_ref[1, e]
        first = (b & 7) < SPLIT
        bins_ref[jnp.where(first, front, BIN - 1 - e + front)] = a + (b << 8)
        return front + first.astype(jnp.int32)

    def step(i, front):
        for u in range(8):
            front = put(i * 8 + u, front)
        return front

    groups = live >> 3
    front = lax.fori_loop(0, groups, step, jnp.int32(0))
    front = lax.fori_loop(groups * 8, live, put, front)
    back = live - front
    count_ref[0] = front
    count_ref[1] = back
    for j in range(TAIL):
        bins_ref[front + j] = 0
        bins_ref[BIN - 1 - back - j] = SPLIT << 8


def spread(strip, t):
    return jnp.broadcast_to(strip[:, t : t + 1], (TILE, TILE))


def row_kernel(own_ref, near_ref, px, py, own_out):
    def row_prepare(r, carry):
        strip = near_ref[r, 256:272, :].astype(f32).T
        for t in range(8):
            px[r * 8 + t] = spread(strip, t)
            py[r * 8 + t] = spread(strip, 8 + t)
        return carry

    lax.fori_loop(0, 8, row_prepare, 0)
    where = own_ref[256:272, :].astype(f32)
    strip = where.T
    for t in range(8):
        dx = spread(strip, t) - where[t : t + 1]
        dy = spread(strip, 8 + t) - where[8 + t : 9 + t]
        block = radial(dx * dx + dy * dy)
        own_out[:, t * TILE : (t + 1) * TILE] = KERNEL_SCALE * lax.dot_general(
            own_ref[t * 32 : (t + 1) * 32, :], block, NT, preferred_element_type=f32
        )


def z_slot(distance):
    low, high = distance & 3, distance >> 2
    return (low << 1) + (high ^ (low & (low >> 1)))


def part_kernel(part, place_ref, count_ref, bins_ref, near_ref, px, py, col_ref, *refs):
    if part == 0:
        row_acc, *col_out, qx, qy, col_acc = refs
        row_acc[...] = jnp.zeros_like(row_acc)
    else:
        row_acc, row_out, *col_out, qx, qy, col_acc = refs
    x_own, y_own, z_own, core_own = place_ref[0], place_ref[1], place_ref[2], place_ref[3]
    tiles = range(SPLIT) if part == 0 else range(SPLIT, 8)
    first, number = tiles[0], len(tiles)
    live = count_ref[part]
    col_acc[...] = jnp.zeros_like(col_acc)

    def col_prepare(r, carry):
        where = col_ref[r, 256:272, :].astype(f32)
        for t in tiles:
            qx[r * 8 + t] = jnp.broadcast_to(where[t : t + 1], (8, TILE))
            qy[r * 8 + t] = jnp.broadcast_to(where[8 + t : 9 + t], (8, TILE))
        return carry

    lax.fori_loop(0, 32, col_prepare, 0)

    def several(start, size):
        results = []
        for u in range(size):
            e = start + u
            both = bins_ref[e if part == 0 else BIN - 1 - e]
            a, b = both & 255, both >> 8
            keep = jnp.where(e < live, 1.0, 0.0).astype(bf16)
            near_slot = ((y_own - (a >> 4)) & 3) + ((((a >> 3) & 1) ^ core_own) << 2)
            z_far = (z_own - (b >> 5)) & 7
            far_slot = (((x_own - (b >> 3)) & 3) << 3) + z_slot(z_far)
            near = near_ref[near_slot, pl.ds(pl.multiple_of((a & 7) * 32, 32), 32), :] * keep
            far = col_ref[far_slot, pl.ds(pl.multiple_of((b & 7) * 32, 32), 32), :] * keep
            a = (near_slot << 3) + (a & 7)
            b = (far_slot << 3) + (b & 7)
            dx = px[a].reshape(16, 8, TILE) - qx[b][None]
            dy = py[a].reshape(16, 8, TILE) - qy[b][None]
            block = radial((dx * dx + dy * dy).reshape(TILE, TILE))
            forward = lax.dot_general(far, block, NT, preferred_element_type=f32)
            backward = lax.dot_general(near, block, NN, preferred_element_type=f32)
            results.append((a, b, forward, backward))
        for a, b, forward, backward in results:
            row_acc[a] += forward
            col_acc[b] += backward

    whole = live // UNROLL

    def body(i, carry):
        several(i * UNROLL, UNROLL)
        return carry

    def tail(i, carry):
        several(whole * UNROLL + i * TAIL, TAIL)
        return carry

    lax.fori_loop(0, whole, body, 0)
    lax.fori_loop(0, (live - whole * UNROLL + TAIL - 1) // TAIL, tail, 0)

    def finish(z, carry):
        for k in range(4):
            for t in range(number):
                total = KERNEL_SCALE * col_acc[k * 64 + z_slot(z) * 8 + first + t]
                col_out[k][(z_own - z) & 7, t * 32 : (t + 1) * 32, :] = total.astype(bf16)
        return carry

    lax.fori_loop(0, 8, finish, 0)
    if part == 1:

        def finish_row(r, carry):
            for t in range(8):
                row_out[r, t * 32 : (t + 1) * 32, :] = (KERNEL_SCALE * row_acc[r * 8 + t]).astype(bf16)
            return carry

        lax.fori_loop(0, 8, finish_row, 0)


def add_kernel(own0, a0, b0, c0, own1, a1, b1, c1, out):
    for z in range(8):
        for rows, parts in ((slice(0, SPLIT * 32), (own0, a0, b0, c0)), (slice(SPLIT * 32, 256), (own1, a1, b1, c1))):
            total = parts[0][z].astype(f32)
            for part in parts[1:]:
                total = total + part[z].astype(f32)
            out[z, rows, :] = total.astype(bf16)


def dot32(former, latter, dims):
    return lax.dot_general(former, latter, dims, precision=HIGHEST, preferred_element_type=f32)


def gram_kernel(direction_ref, residual_ref, own_ref, row_ref, col_ref, image_ref, gram_ref):
    for t in range(8):
        here = slice(t * 32, (t + 1) * 32)
        lanes = slice(t * TILE, (t + 1) * TILE)
        total = NUGGET * direction_ref[:, lanes] + own_ref[:, lanes]
        for part in range(row_ref.shape[0]):
            total = total + row_ref[part, here, :].astype(f32)
        for part in range(col_ref.shape[0]):
            total = total + col_ref[part, here, :].astype(f32)
        image_ref[:, lanes] = total
    direction, residual, image = direction_ref[...], residual_ref[...], image_ref[...]
    gram_ref[0:32, 0:32] = dot32(direction, image, NT)
    gram_ref[0:32, 32:64] = dot32(direction, residual, NT)
    gram_ref[0:32, 64:96] = dot32(residual, residual, NT)
    gram_ref[0:32, 96:128] = dot32(residual, image, NT)
    square = dot32(image, image, NT)
    for t in range(4):
        gram_ref[32:40, t * 32 : (t + 1) * 32] = square[t * 8 : (t + 1) * 8]


def solve_kernel(gram_ref, solution_ref, residual_ref, direction_ref, image_ref, solution_out, residual_out, direction_out):
    gram = gram_ref[...]
    curvature, crossing = gram[0:32, 0:32], gram[0:32, 32:64]
    norm_old, mixed = gram[0:32, 64:96], gram[0:32, 96:128]
    square = jnp.concatenate([gram[32:40, t * 32 : (t + 1) * 32] for t in range(4)], 0)
    row = lax.broadcasted_iota(jnp.int32, (32, 64), 0)
    lane = lax.broadcasted_iota(jnp.int32, (32, 64), 1)
    unit = jnp.where(row[:, :32] == lane[:, :32], 1.0, 0.0).astype(f32)
    first = jnp.concatenate([0.5 * (curvature + curvature.T), crossing], 1)
    second = jnp.concatenate([0.5 * (norm_old + norm_old.T), unit], 1)

    def eliminate(table, k):
        pivot_row = table[k : k + 1, :] / table[k : k + 1, k : k + 1]
        return jnp.where(row == k, pivot_row, table - table[:, k : k + 1] * pivot_row)

    for k in range(32):
        first, second = eliminate(first, k), eliminate(second, k)
    alpha, inverse = first[:, 32:64], second[:, 32:64]
    cross = dot32(mixed, alpha, NN)
    norm_new = 0.5 * (norm_old + norm_old.T) - cross - cross.T + dot32(alpha, dot32(square, alpha, NN), TN)
    beta = dot32(inverse, norm_new, NN)
    direction = direction_ref[...]
    residual_next = residual_ref[...] - dot32(alpha, image_ref[...], TN)
    residual_out[...] = residual_next
    solution_out[...] = solution_ref[...] + dot32(alpha, direction, TN)
    direction_out[...] = residual_next + dot32(beta, direction, TN)


def shifts(value, axis, size):
    return [lax.ppermute(value, axis, [(i, (i + k) % size) for i in range(size)]) for k in range(1, size)]


def swap(value):
    return lax.ppermute(value, "core", [(0, 1), (1, 0)])


def on_device(solution_field, residual, direction, positions, tile_pairs, pair_count):
    shape = jax.ShapeDtypeStruct
    own_points = direction.shape[1]
    packed = pl.pallas_call(
        pack_kernel, out_shape=shape((272, TILE), bf16), in_specs=[VMEM] * 2, out_specs=VMEM, compiler_params=SMALL, name="pack"
    )(direction, positions)
    def moved(value, axis, size, shift):
        return lax.ppermute(value, axis, [(i, (i + shift) % size) for i in range(size)])

    other = swap(packed)
    pair = jnp.stack([packed, moved(packed, "z", 8, 4)])
    one, two, back = [moved(pair, "z", 8, shift) for shift in (1, 2, -1)]
    pair_below, pair_above = moved(pair, "x", 4, 1), moved(pair, "x", 4, -1)
    rest = jnp.concatenate([one, two, back], 0)
    rest_below, rest_above = moved(rest, "x", 4, 1), moved(rest, "x", 4, -1)
    far_below = moved(jnp.concatenate([pair_below[:1], rest_below[:3]], 0), "x", 4, 1)
    far_above = moved(jnp.concatenate([pair_above[1:], rest_above[3:]], 0), "x", 4, -1)
    col_all = jnp.concatenate(
        [pair, rest, pair_below, rest_below, far_below[:1], far_above[:1], far_below[1:], far_above[1:], pair_above, rest_above], 0
    )
    chip, pair_below = lax.optimization_barrier((jnp.stack([packed, other]), pair_below))
    around = shifts(chip, "y", 4)
    row_all = jnp.concatenate([v[:1] for v in [chip] + around] + [v[1:] for v in [chip] + around], 0)
    place = jnp.stack([lax.axis_index(name) for name in ("x", "y", "z", "core")]).astype(jnp.int32)
    bins, counts = pl.pallas_call(
        bin_kernel,
        out_shape=(shape((BIN,), jnp.int32), shape((2,), jnp.int32)),
        in_specs=[SMEM, SMEM, VMEM],
        out_specs=(SMEM, SMEM),
        compiler_params=SMALL,
        name="bins",
    )(pair_count, tile_pairs, rest_above[0, :16])
    spread_shape = shape((64, TILE, TILE), f32)
    px, py, own_product = pl.pallas_call(
        row_kernel,
        out_shape=(spread_shape, spread_shape, shape((PROBES, own_points), f32)),
        in_specs=[VMEM] * 2,
        out_specs=(VMEM,) * 3,
        compiler_params=PARAMS,
        name="rows",
    )(packed, row_all)
    acc = shape((64, PROBES, TILE), f32)
    scratch = [pltpu.VMEM((256, 8, TILE), f32), pltpu.VMEM((256, 8, TILE), f32), pltpu.VMEM((256, PROBES, TILE), f32)]

    def blocks(number):
        return (shape((8, number * 32, TILE), bf16),) * 4

    def sent(col_out):
        return [lax.ppermute(col_out[k], "x", [(i, (i - k) % 4) for i in range(4)]) for k in range(1, 4)]

    row_acc, *col_first = pl.pallas_call(
        functools.partial(part_kernel, 0),
        out_shape=(acc,) + blocks(SPLIT),
        in_specs=[SMEM] * 3 + [VMEM] * 4,
        out_specs=(VMEM,) * 5,
        scratch_shapes=scratch,
        compiler_params=PARAMS,
        name="pairs_first",
    )(place, counts, bins, row_all, px, py, col_all)
    row_sum, *col_second = pl.pallas_call(
        functools.partial(part_kernel, 1),
        out_shape=(shape((8, 256, TILE), bf16),) + blocks(8 - SPLIT),
        in_specs=[SMEM] * 3 + [VMEM] * 5,
        out_specs=(VMEM,) * 5,
        scratch_shapes=scratch,
        compiler_params=PARAMS,
        name="pairs_second",
    )(place, counts, bins, row_all, px, py, col_all, row_acc)
    sums = pl.pallas_call(
        add_kernel,
        out_shape=shape((8, 256, TILE), bf16),
        in_specs=[VMEM] * 8,
        out_specs=VMEM,
        compiler_params=PARAMS,
        name="add",
    )(col_first[0], *sent(col_first), col_second[0], *sent(col_second))
    col_parts = lax.all_to_all(sums, "z", 0, 0)
    half = (row_sum[:4].astype(f32) + swap(row_sum[4:]).astype(f32)).astype(bf16)
    row_parts = [half[0]] + [
        lax.ppermute(half[k], "y", [(i, (i - k) % 4) for i in range(4)]) for k in range(1, 4)
    ]
    row_parts = jnp.stack(row_parts)
    image, gram = pl.pallas_call(
        gram_kernel,
        out_shape=(shape((PROBES, own_points), f32), shape((40, TILE), f32)),
        in_specs=[VMEM] * 5,
        out_specs=(VMEM, VMEM),
        compiler_params=PARAMS,
        name="gram",
    )(direction, residual, own_product, row_parts, col_parts)
    gram = gram + swap(gram)
    gram = sum(shifts(gram, "y", 4), gram)
    gram = sum(shifts(gram, "x", 4), gram)
    gram = gram + lax.ppermute(gram, "z", [(i, (i + 4) % 8) for i in range(8)])
    gram = sum(shifts(gram, "z", 8)[:3], gram)
    return pl.pallas_call(
        solve_kernel,
        out_shape=(shape((PROBES, own_points), f32),) * 3,
        in_specs=[VMEM] * 5,
        out_specs=(VMEM,) * 3,
        compiler_params=PARAMS,
        name="solve",
    )(gram, solution_field, residual, direction, image)


def solution(mesh):
    fine = Mesh(np.asarray(mesh.devices).reshape(8, 4, 4, 2), ("z", "x", "y", "core"))
    points = P(None, ("z", "x", "y", "core"))
    return jax.shard_map(
        on_device,
        mesh=fine,
        in_specs=(points,) * 5 + (P(("z", "x", "y", "core")),),
        out_specs=(points,) * 3,
        check_vma=False,
    )
```

```python
import functools

import jax
import jax.numpy as jnp
import numpy as np
from jax import lax
from jax.experimental import pallas as pl
from jax.experimental.pallas import tpu as pltpu
from jax.sharding import Mesh
from jax.sharding import PartitionSpec as P

TILE = 128
PROBES = 32
UNROLL = 32
TAIL = 8
SPLIT = 6
BIN = 1536 + 2 * UNROLL
NUGGET = 2.0
KERNEL_SCALE = 0.1
HIGHEST = lax.Precision.HIGHEST
f32, bf16 = jnp.float32, jnp.bfloat16
VMEM = pl.BlockSpec(memory_space=pltpu.VMEM)
SMEM = pl.BlockSpec(memory_space=pltpu.SMEM)
NT = (((1,), (1,)), ((), ()))
NN = (((1,), (0,)), ((), ()))
TN = (((0,), (0,)), ((), ()))
PARAMS = pltpu.CompilerParams(vmem_limit_bytes=16 * 2**20)
SMALL = pltpu.CompilerParams(vmem_limit_bytes=4 * 2**20)


def pack_kernel(direction_ref, positions_ref, packed_ref):
    for t in range(8):
        packed_ref[t * 32 : (t + 1) * 32, :] = direction_ref[:, t * TILE : (t + 1) * TILE].astype(bf16)
    where = positions_ref[...].astype(f32)
    rows = [where[d : d + 1, t * TILE : (t + 1) * TILE] for d in range(2) for t in range(8)]
    packed_ref[256:272, :] = jnp.concatenate(rows, 0).astype(bf16)


def radial(square):
    distance = pl.reciprocal(lax.rsqrt(square), approx=True)
    remain = jnp.maximum(1.0 - distance, 0.0)
    remain2 = remain * remain
    return ((remain2 * remain2) * (1.25 - remain)).astype(bf16)


def bin_kernel(live_ref, pairs_ref, after_ref, bins_ref, count_ref):
    live = live_ref[0]

    def put(e, front):
        a, b = pairs_ref[0, e], pairs_ref[1, e]
        first = (b & 7) < SPLIT
        bins_ref[jnp.where(first, front, BIN - 1 - e + front)] = a + (b << 8)
        return front + first.astype(jnp.int32)

    def step(i, front):
        for u in range(8):
            front = put(i * 8 + u, front)
        return front

    groups = live >> 3
    front = lax.fori_loop(0, groups, step, jnp.int32(0))
    front = lax.fori_loop(groups * 8, live, put, front)
    back = live - front
    count_ref[0] = front
    count_ref[1] = back
    for j in range(TAIL):
        bins_ref[front + j] = 0
        bins_ref[BIN - 1 - back - j] = SPLIT << 8


def spread(strip, t):
    return jnp.broadcast_to(strip[:, t : t + 1], (TILE, TILE))


def row_kernel(own_ref, near_ref, after_ref, px, py, own_out):
    def row_prepare(r, carry):
        strip = near_ref[r, 256:272, :].astype(f32).T
        for t in range(8):
            px[r * 8 + t] = spread(strip, t)
            py[r * 8 + t] = spread(strip, 8 + t)
        return carry

    lax.fori_loop(0, 8, row_prepare, 0)
    where = own_ref[256:272, :].astype(f32)
    strip = where.T
    for t in range(8):
        dx = spread(strip, t) - where[t : t + 1]
        dy = spread(strip, 8 + t) - where[8 + t : 9 + t]
        block = radial(dx * dx + dy * dy)
        own_out[:, t * TILE : (t + 1) * TILE] = KERNEL_SCALE * lax.dot_general(
            own_ref[t * 32 : (t + 1) * 32, :], block, NT, preferred_element_type=f32
        )


def z_slot(distance):
    low, high = distance & 3, distance >> 2
    return (low << 1) + (high ^ (low & (low >> 1)))


def part_kernel(part, place_ref, count_ref, bins_ref, near_ref, px, py, col_ref, *refs):
    if part == 0:
        row_acc, *col_out, qx, qy, col_acc = refs
        row_acc[...] = jnp.zeros_like(row_acc)
    else:
        row_acc, row_out, *col_out, qx, qy, col_acc = refs
    x_own, y_own, z_own, core_own = place_ref[0], place_ref[1], place_ref[2], place_ref[3]
    tiles = range(SPLIT) if part == 0 else range(SPLIT, 8)
    first, number = tiles[0], len(tiles)
    live = count_ref[part]
    col_acc[...] = jnp.zeros_like(col_acc)

    def col_prepare(r, carry):
        where = col_ref[r, 256:272, :].astype(f32)
        for t in tiles:
            qx[r * 8 + t] = jnp.broadcast_to(where[t : t + 1], (8, TILE))
            qy[r * 8 + t] = jnp.broadcast_to(where[8 + t : 9 + t], (8, TILE))
        return carry

    lax.fori_loop(0, 32, col_prepare, 0)

    def several(start, size, masked):
        results = []
        for u in range(size):
            e = start + u
            both = bins_ref[e if part == 0 else BIN - 1 - e]
            a, b = both & 255, both >> 8
            near_slot = ((y_own - (a >> 4)) & 3) + ((((a >> 3) & 1) ^ core_own) << 2)
            z_far = (z_own - (b >> 5)) & 7
            far_slot = (((x_own - (b >> 3)) & 3) << 3) + z_slot(z_far)
            near = near_ref[near_slot, pl.ds(pl.multiple_of((a & 7) * 32, 32), 32), :]
            far = col_ref[far_slot, pl.ds(pl.multiple_of((b & 7) * 32, 32), 32), :]
            if masked:
                keep = jnp.where(e < live, 1.0, 0.0).astype(bf16)
                near, far = near * keep, far * keep
            a = (near_slot << 3) + (a & 7)
            b = (far_slot << 3) + (b & 7)
            dx = px[a].reshape(16, 8, TILE) - qx[b][None]
            dy = py[a].reshape(16, 8, TILE) - qy[b][None]
            block = radial((dx * dx + dy * dy).reshape(TILE, TILE))
            forward = lax.dot_general(far, block, NT, preferred_element_type=f32)
            backward = lax.dot_general(near, block, NN, preferred_element_type=f32)
            results.append((a, b, forward, backward))
        for a, b, forward, backward in results:
            row_acc[a] += forward
            col_acc[b] += backward

    whole = live // UNROLL

    def body(i, carry):
        several(i * UNROLL, UNROLL, False)
        return carry

    def tail(i, carry):
        several(whole * UNROLL + i * TAIL, TAIL, True)
        return carry

    lax.fori_loop(0, whole, body, 0)
    lax.fori_loop(0, (live - whole * UNROLL + TAIL - 1) // TAIL, tail, 0)

    def finish(z, carry):
        for k in range(4):
            for t in range(number):
                total = KERNEL_SCALE * col_acc[k * 64 + z_slot(z) * 8 + first + t]
                col_out[k][(z_own - z) & 7, t * 32 : (t + 1) * 32, :] = total.astype(bf16)
        return carry

    lax.fori_loop(0, 8, finish, 0)
    if part == 1:

        def finish_row(r, carry):
            for t in range(8):
                row_out[r, t * 32 : (t + 1) * 32, :] = (KERNEL_SCALE * row_acc[r * 8 + t]).astype(bf16)
            return carry

        lax.fori_loop(0, 8, finish_row, 0)


def add_kernel(own0, a0, b0, c0, own1, a1, b1, c1, out):
    for z in range(8):
        for rows, parts in ((slice(0, SPLIT * 32), (own0, a0, b0, c0)), (slice(SPLIT * 32, 256), (own1, a1, b1, c1))):
            total = parts[0][z].astype(f32)
            for part in parts[1:]:
                total = total + part[z].astype(f32)
            out[z, rows, :] = total.astype(bf16)


def dot32(former, latter, dims):
    return lax.dot_general(former, latter, dims, precision=HIGHEST, preferred_element_type=f32)


def gram_kernel(direction_ref, residual_ref, own_ref, row_ref, col_ref, image_ref, gram_ref):
    for t in range(8):
        here = slice(t * 32, (t + 1) * 32)
        lanes = slice(t * TILE, (t + 1) * TILE)
        total = NUGGET * direction_ref[:, lanes] + own_ref[:, lanes]
        for part in range(row_ref.shape[0]):
            total = total + row_ref[part, here, :].astype(f32)
        for part in range(col_ref.shape[0]):
            total = total + col_ref[part, here, :].astype(f32)
        image_ref[:, lanes] = total
    direction, residual, image = direction_ref[...], residual_ref[...], image_ref[...]
    gram_ref[0:32, 0:32] = dot32(direction, image, NT)
    gram_ref[0:32, 32:64] = dot32(direction, residual, NT)
    gram_ref[0:32, 64:96] = dot32(residual, residual, NT)
    gram_ref[0:32, 96:128] = dot32(residual, image, NT)
    square = dot32(image, image, NT)
    for t in range(4):
        gram_ref[32:40, t * 32 : (t + 1) * 32] = square[t * 8 : (t + 1) * 8]


def solve_kernel(gram_ref, solution_ref, residual_ref, direction_ref, image_ref, solution_out, residual_out, direction_out):
    gram = gram_ref[...]
    curvature, crossing = gram[0:32, 0:32], gram[0:32, 32:64]
    norm_old, mixed = gram[0:32, 64:96], gram[0:32, 96:128]
    square = jnp.concatenate([gram[32:40, t * 32 : (t + 1) * 32] for t in range(4)], 0)
    row = lax.broadcasted_iota(jnp.int32, (32, 64), 0)
    lane = lax.broadcasted_iota(jnp.int32, (32, 64), 1)
    unit = jnp.where(row[:, :32] == lane[:, :32], 1.0, 0.0).astype(f32)
    first = jnp.concatenate([0.5 * (curvature + curvature.T), crossing], 1)
    second = jnp.concatenate([0.5 * (norm_old + norm_old.T), unit], 1)

    def eliminate(table, k):
        pivot_row = table[k : k + 1, :] / table[k : k + 1, k : k + 1]
        return jnp.where(row == k, pivot_row, table - table[:, k : k + 1] * pivot_row)

    for k in range(32):
        first, second = eliminate(first, k), eliminate(second, k)
    alpha, inverse = first[:, 32:64], second[:, 32:64]
    cross = dot32(mixed, alpha, NN)
    norm_new = 0.5 * (norm_old + norm_old.T) - cross - cross.T + dot32(alpha, dot32(square, alpha, NN), TN)
    beta = dot32(inverse, norm_new, NN)
    direction = direction_ref[...]
    residual_next = residual_ref[...] - dot32(alpha, image_ref[...], TN)
    residual_out[...] = residual_next
    solution_out[...] = solution_ref[...] + dot32(alpha, direction, TN)
    direction_out[...] = residual_next + dot32(beta, direction, TN)


def shifts(value, axis, size):
    return [lax.ppermute(value, axis, [(i, (i + k) % size) for i in range(size)]) for k in range(1, size)]


def swap(value):
    return lax.ppermute(value, "core", [(0, 1), (1, 0)])


def on_device(solution_field, residual, direction, positions, tile_pairs, pair_count):
    shape = jax.ShapeDtypeStruct
    own_points = direction.shape[1]
    packed = pl.pallas_call(
        pack_kernel, out_shape=shape((272, TILE), bf16), in_specs=[VMEM] * 2, out_specs=VMEM, compiler_params=SMALL, name="pack"
    )(direction, positions)
    def moved(value, axis, size, shift):
        return lax.ppermute(value, axis, [(i, (i + shift) % size) for i in range(size)])

    row_half = jnp.stack([packed] + shifts(packed, "y", 4))
    pair = jnp.stack([packed, moved(packed, "z", 8, 4)])
    one, two, back = [moved(pair, "z", 8, shift) for shift in (1, 2, -1)]
    pair_below, pair_above = moved(pair, "x", 4, 1), moved(pair, "x", 4, -1)
    rest = jnp.concatenate([one, two, back], 0)
    row_half, rest = lax.optimization_barrier((row_half, rest))
    rest_below, rest_above = moved(rest, "x", 4, 1), moved(rest, "x", 4, -1)
    far_below = moved(jnp.concatenate([pair_below[:1], rest_below[:3]], 0), "x", 4, 1)
    far_above = moved(jnp.concatenate([pair_above[1:], rest_above[3:]], 0), "x", 4, -1)
    col_all = jnp.concatenate(
        [pair, rest, pair_below, rest_below, far_below[:1], far_above[:1], far_below[1:], far_above[1:], pair_above, rest_above], 0
    )
    row_all = jnp.concatenate([row_half, swap(row_half)], 0)
    place = jnp.stack([lax.axis_index(name) for name in ("x", "y", "z", "core")]).astype(jnp.int32)
    bins, counts = pl.pallas_call(
        bin_kernel,
        out_shape=(shape((BIN,), jnp.int32), shape((2,), jnp.int32)),
        in_specs=[SMEM, SMEM, VMEM],
        out_specs=(SMEM, SMEM),
        compiler_params=SMALL,
        name="bins",
    )(pair_count, tile_pairs, pair_above[0, :16])
    spread_shape = shape((64, TILE, TILE), f32)
    px, py, own_product = pl.pallas_call(
        row_kernel,
        out_shape=(spread_shape, spread_shape, shape((PROBES, own_points), f32)),
        in_specs=[VMEM] * 3,
        out_specs=(VMEM,) * 3,
        compiler_params=PARAMS,
        name="rows",
    )(packed, row_all, rest_above[0, :16])
    acc = shape((64, PROBES, TILE), f32)
    scratch = [pltpu.VMEM((256, 8, TILE), f32), pltpu.VMEM((256, 8, TILE), f32), pltpu.VMEM((256, PROBES, TILE), f32)]

    def blocks(number):
        return (shape((8, number * 32, TILE), bf16),) * 4

    def sent(col_out):
        return [lax.ppermute(col_out[k], "x", [(i, (i - k) % 4) for i in range(4)]) for k in range(1, 4)]

    row_acc, *col_first = pl.pallas_call(
        functools.partial(part_kernel, 0),
        out_shape=(acc,) + blocks(SPLIT),
        in_specs=[SMEM] * 3 + [VMEM] * 4,
        out_specs=(VMEM,) * 5,
        scratch_shapes=scratch,
        compiler_params=PARAMS,
        name="pairs_first",
    )(place, counts, bins, row_all, px, py, col_all)
    row_sum, *col_second = pl.pallas_call(
        functools.partial(part_kernel, 1),
        out_shape=(shape((8, 256, TILE), bf16),) + blocks(8 - SPLIT),
        in_specs=[SMEM] * 3 + [VMEM] * 5,
        out_specs=(VMEM,) * 5,
        scratch_shapes=scratch,
        compiler_params=PARAMS,
        name="pairs_second",
    )(place, counts, bins, row_all, px, py, col_all, row_acc)
    sums = pl.pallas_call(
        add_kernel,
        out_shape=shape((8, 256, TILE), bf16),
        in_specs=[VMEM] * 8,
        out_specs=VMEM,
        compiler_params=PARAMS,
        name="add",
    )(col_first[0], *sent(col_first), col_second[0], *sent(col_second))
    col_parts = lax.all_to_all(sums, "z", 0, 0)
    half = (row_sum[:4].astype(f32) + swap(row_sum[4:]).astype(f32)).astype(bf16)
    row_parts = [half[0]] + [
        lax.ppermute(half[k], "y", [(i, (i - k) % 4) for i in range(4)]) for k in range(1, 4)
    ]
    row_parts = jnp.stack(row_parts)
    image, gram = pl.pallas_call(
        gram_kernel,
        out_shape=(shape((PROBES, own_points), f32), shape((40, TILE), f32)),
        in_specs=[VMEM] * 5,
        out_specs=(VMEM, VMEM),
        compiler_params=PARAMS,
        name="gram",
    )(direction, residual, own_product, row_parts, col_parts)
    gram = gram + swap(gram)
    gram = sum(shifts(gram, "y", 4), gram)
    gram = sum(shifts(gram, "x", 4), gram)
    gram = gram + lax.ppermute(gram, "z", [(i, (i + 4) % 8) for i in range(8)])
    gram = sum(shifts(gram, "z", 8)[:3], gram)
    return pl.pallas_call(
        solve_kernel,
        out_shape=(shape((PROBES, own_points), f32),) * 3,
        in_specs=[VMEM] * 5,
        out_specs=(VMEM,) * 3,
        compiler_params=PARAMS,
        name="solve",
    )(gram, solution_field, residual, direction, image)


def solution(mesh):
    fine = Mesh(np.asarray(mesh.devices).reshape(8, 4, 4, 2), ("z", "x", "y", "core"))
    points = P(None, ("z", "x", "y", "core"))
    return jax.shard_map(
        on_device,
        mesh=fine,
        in_specs=(points,) * 5 + (P(("z", "x", "y", "core")),),
        out_specs=(points,) * 3,
        check_vma=False,
    )
```

```python
import functools

import jax
import jax.numpy as jnp
import numpy as np
from jax import lax
from jax.experimental import pallas as pl
from jax.experimental.pallas import tpu as pltpu
from jax.sharding import Mesh
from jax.sharding import PartitionSpec as P

TILE = 128
PROBES = 32
UNROLL = 32
TAIL = 8
PARTS = (2, 1, 1)
LIST = 1536 + UNROLL
NUGGET = 2.0
KERNEL_SCALE = 0.1
HIGHEST = lax.Precision.HIGHEST
f32, bf16 = jnp.float32, jnp.bfloat16
VMEM = pl.BlockSpec(memory_space=pltpu.VMEM)
SMEM = pl.BlockSpec(memory_space=pltpu.SMEM)
NT = (((1,), (1,)), ((), ()))
NN = (((1,), (0,)), ((), ()))
TN = (((0,), (0,)), ((), ()))
PARAMS = pltpu.CompilerParams(vmem_limit_bytes=16 * 2**20)
SMALL = pltpu.CompilerParams(vmem_limit_bytes=4 * 2**20)


def pack_kernel(direction_ref, positions_ref, packed_ref):
    for t in range(8):
        packed_ref[t * 32 : (t + 1) * 32, :] = direction_ref[:, t * TILE : (t + 1) * TILE].astype(bf16)
    where = positions_ref[...].astype(f32)
    rows = [where[d : d + 1, t * TILE : (t + 1) * TILE] for d in range(2) for t in range(8)]
    packed_ref[256:272, :] = jnp.concatenate(rows, 0).astype(bf16)


def radial(square):
    distance = pl.reciprocal(lax.rsqrt(square), approx=True)
    remain = jnp.maximum(1.0 - distance, 0.0)
    remain2 = remain * remain
    return ((remain2 * remain2) * (1.25 - remain)).astype(bf16)


def bin_kernel(live_ref, entries_ref, after_ref, bins_ref, count_ref):
    live = live_ref[0]

    def put(e, ends):
        first, second = ends
        entry = entries_ref[e]
        bins_ref[first] = entry
        bins_ref[LIST + second] = entry
        bins_ref[2 * LIST + e - first - second] = entry
        return first + ((entry >> 16) & 1), second + ((entry >> 17) & 1)

    def step(i, ends):
        for u in range(8):
            ends = put(i * 8 + u, ends)
        return ends

    groups = live >> 3
    ends = lax.fori_loop(0, groups, step, (jnp.int32(0), jnp.int32(0)))
    first, second = lax.fori_loop(groups * 8, live, put, ends)
    for part, end in enumerate((first, second, live - first - second)):
        count_ref[part] = end
        for j in range(TAIL):
            bins_ref[part * LIST + end + j] = 0


def spread(strip, t):
    return jnp.broadcast_to(strip[:, t : t + 1], (TILE, TILE))


def row_kernel(own_ref, near_ref, px, py, own_out):
    def row_prepare(r, carry):
        strip = near_ref[r, 256:272, :].astype(f32).T
        for t in range(8):
            px[r * 8 + t] = spread(strip, t)
            py[r * 8 + t] = spread(strip, 8 + t)
        return carry

    lax.fori_loop(0, 8, row_prepare, 0)
    where = own_ref[256:272, :].astype(f32)
    strip = where.T
    for t in range(8):
        dx = spread(strip, t) - where[t : t + 1]
        dy = spread(strip, 8 + t) - where[8 + t : 9 + t]
        block = radial(dx * dx + dy * dy)
        own_out[:, t * TILE : (t + 1) * TILE] = KERNEL_SCALE * lax.dot_general(
            own_ref[t * 32 : (t + 1) * 32, :], block, NT, preferred_element_type=f32
        )


def z_slot(distance):
    low, high = distance & 3, distance >> 2
    return (low << 1) + (high ^ (low & (low >> 1)))


def part_kernel(part, place_ref, count_ref, bins_ref, near_ref, px, py, col_ref, *refs):
    if part == 0:
        row_acc, *col_out, qx, qy, col_acc = refs
        row_acc[...] = jnp.zeros_like(row_acc)
    elif part == 1:
        before, row_acc, *col_out, qx, qy, col_acc = refs
        row_acc[...] = before[...]
    else:
        before, row_acc, row_out, *col_out, qx, qy, col_acc = refs
        row_acc[...] = before[...]
    z_own = place_ref[0]
    live = count_ref[part]
    col_acc[...] = jnp.zeros_like(col_acc)

    def col_prepare(r, carry):
        where = col_ref[r, 256:272, :].astype(f32)
        for t in range(8):
            qx[r * 8 + t] = jnp.broadcast_to(where[t : t + 1], (8, TILE))
            qy[r * 8 + t] = jnp.broadcast_to(where[8 + t : 9 + t], (8, TILE))
        return carry

    lax.fori_loop(0, 8 * PARTS[part], col_prepare, 0)

    def several(start, size, masked):
        results = []
        for u in range(size):
            e = start + u
            entry = bins_ref[part * LIST + e]
            a, b = entry & 255, (entry >> 8) & 255
            near = near_ref[a >> 3, pl.ds(pl.multiple_of((a & 7) * 32, 32), 32), :]
            far = col_ref[b >> 3, pl.ds(pl.multiple_of((b & 7) * 32, 32), 32), :]
            if masked:
                keep = jnp.where(e < live, 1.0, 0.0).astype(bf16)
                near, far = near * keep, far * keep
            dx = px[a].reshape(16, 8, TILE) - qx[b][None]
            dy = py[a].reshape(16, 8, TILE) - qy[b][None]
            block = radial((dx * dx + dy * dy).reshape(TILE, TILE))
            forward = lax.dot_general(far, block, NT, preferred_element_type=f32)
            backward = lax.dot_general(near, block, NN, preferred_element_type=f32)
            results.append((a, b, forward, backward))
        for a, b, forward, backward in results:
            row_acc[a] += forward
            col_acc[b] += backward

    whole = live // UNROLL

    def body(i, carry):
        several(i * UNROLL, UNROLL, False)
        return carry

    def tail(i, carry):
        several(whole * UNROLL + i * TAIL, TAIL, True)
        return carry

    lax.fori_loop(0, whole, body, 0)
    lax.fori_loop(0, (live - whole * UNROLL + TAIL - 1) // TAIL, tail, 0)

    def finish(z, carry):
        for k in range(PARTS[part]):
            for t in range(8):
                total = KERNEL_SCALE * col_acc[k * 64 + z_slot(z) * 8 + t]
                col_out[k][(z_own - z) & 7, t * 32 : (t + 1) * 32, :] = total.astype(bf16)
        return carry

    lax.fori_loop(0, 8, finish, 0)
    if part == 2:

        def finish_row(r, carry):
            for t in range(8):
                row_out[r, t * 32 : (t + 1) * 32, :] = (KERNEL_SCALE * row_acc[r * 8 + t]).astype(bf16)
            return carry

        lax.fori_loop(0, 8, finish_row, 0)


def add_kernel(own, below, far, above, out):
    for z in range(8):
        total = (own[z].astype(f32) + below[z].astype(f32)) + (far[z].astype(f32) + above[z].astype(f32))
        out[z] = total.astype(bf16)


def dot32(former, latter, dims):
    return lax.dot_general(former, latter, dims, precision=HIGHEST, preferred_element_type=f32)


def gram_kernel(direction_ref, residual_ref, own_ref, row_ref, col_ref, image_ref, gram_ref):
    for t in range(8):
        here = slice(t * 32, (t + 1) * 32)
        lanes = slice(t * TILE, (t + 1) * TILE)
        total = NUGGET * direction_ref[:, lanes] + own_ref[:, lanes]
        for part in range(row_ref.shape[0]):
            total = total + row_ref[part, here, :].astype(f32)
        for part in range(col_ref.shape[0]):
            total = total + col_ref[part, here, :].astype(f32)
        image_ref[:, lanes] = total
    direction, residual, image = direction_ref[...], residual_ref[...], image_ref[...]
    gram_ref[0:32, 0:32] = dot32(direction, image, NT)
    gram_ref[0:32, 32:64] = dot32(direction, residual, NT)
    gram_ref[0:32, 64:96] = dot32(residual, residual, NT)
    gram_ref[0:32, 96:128] = dot32(residual, image, NT)
    square = dot32(image, image, NT)
    for t in range(4):
        gram_ref[32:40, t * 32 : (t + 1) * 32] = square[t * 8 : (t + 1) * 8]


def solve_kernel(gram_ref, solution_ref, residual_ref, direction_ref, image_ref, solution_out, residual_out, direction_out):
    gram = gram_ref[...]
    curvature, crossing = gram[0:32, 0:32], gram[0:32, 32:64]
    norm_old, mixed = gram[0:32, 64:96], gram[0:32, 96:128]
    square = jnp.concatenate([gram[32:40, t * 32 : (t + 1) * 32] for t in range(4)], 0)
    row = lax.broadcasted_iota(jnp.int32, (32, 64), 0)
    lane = lax.broadcasted_iota(jnp.int32, (32, 64), 1)
    unit = jnp.where(row[:, :32] == lane[:, :32], 1.0, 0.0).astype(f32)
    first = jnp.concatenate([0.5 * (curvature + curvature.T), crossing], 1)
    second = jnp.concatenate([0.5 * (norm_old + norm_old.T), unit], 1)

    def eliminate(table, k):
        pivot_row = table[k : k + 1, :] / table[k : k + 1, k : k + 1]
        return jnp.where(row == k, pivot_row, table - table[:, k : k + 1] * pivot_row)

    for k in range(32):
        first, second = eliminate(first, k), eliminate(second, k)
    alpha, inverse = first[:, 32:64], second[:, 32:64]
    cross = dot32(mixed, alpha, NN)
    norm_new = 0.5 * (norm_old + norm_old.T) - cross - cross.T + dot32(alpha, dot32(square, alpha, NN), TN)
    beta = dot32(inverse, norm_new, NN)
    direction = direction_ref[...]
    residual_next = residual_ref[...] - dot32(alpha, image_ref[...], TN)
    residual_out[...] = residual_next
    solution_out[...] = solution_ref[...] + dot32(alpha, direction, TN)
    direction_out[...] = residual_next + dot32(beta, direction, TN)


def shifts(value, axis, size):
    return [lax.ppermute(value, axis, [(i, (i + k) % size) for i in range(size)]) for k in range(1, size)]


def swap(value):
    return lax.ppermute(value, "core", [(0, 1), (1, 0)])


def on_device(solution_field, residual, direction, positions, tile_pairs, pair_count):
    shape = jax.ShapeDtypeStruct
    own_points = direction.shape[1]
    packed = pl.pallas_call(
        pack_kernel, out_shape=shape((272, TILE), bf16), in_specs=[VMEM] * 2, out_specs=VMEM, compiler_params=SMALL, name="pack"
    )(direction, positions)
    def moved(value, axis, size, shift):
        return lax.ppermute(value, axis, [(i, (i + shift) % size) for i in range(size)])

    row_half = jnp.stack([packed] + shifts(packed, "y", 4))
    pair = jnp.stack([packed, moved(packed, "z", 8, 4)])
    one, two, back = [moved(pair, "z", 8, shift) for shift in (1, 2, -1)]
    pair_below, pair_above = moved(pair, "x", 4, 1), moved(pair, "x", 4, -1)
    rest = jnp.concatenate([one, two, back], 0)
    row_half, rest = lax.optimization_barrier((row_half, rest))
    rest_below, rest_above = moved(rest, "x", 4, 1), moved(rest, "x", 4, -1)
    row_all = jnp.concatenate([row_half, swap(row_half)], 0)
    x_own, y_own, z_own, core_own = [lax.axis_index(name).astype(jnp.int32) for name in ("x", "y", "z", "core")]
    place = z_own.reshape(1)
    a, b = tile_pairs[0], tile_pairs[1]
    near_slot = ((y_own - (a >> 4)) & 3) + ((((a >> 3) & 1) ^ core_own) << 2)
    x_far = (x_own - (b >> 3)) & 3
    far_slot = z_slot((z_own - (b >> 5)) & 7) + jnp.where(x_far == 3, 8, 0)
    entries = (near_slot << 3) + (a & 7) + (far_slot << 11) + ((b & 7) << 8)
    entries = entries + ((x_far & 1) << 16) + jnp.where(x_far == 2, 1 << 17, 0)
    bins, counts = pl.pallas_call(
        bin_kernel,
        out_shape=(shape((3 * LIST,), jnp.int32), shape((3,), jnp.int32)),
        in_specs=[SMEM, SMEM, VMEM],
        out_specs=(SMEM, SMEM),
        compiler_params=SMALL,
        name="bins",
    )(pair_count, entries, pair_above[0, :16])
    spread_shape = shape((64, TILE, TILE), f32)
    px, py, own_product = pl.pallas_call(
        row_kernel,
        out_shape=(spread_shape, spread_shape, shape((PROBES, own_points), f32)),
        in_specs=[VMEM] * 2,
        out_specs=(VMEM,) * 3,
        compiler_params=PARAMS,
        name="rows",
    )(packed, row_all)
    rest_below, rest_above, bins, px = lax.optimization_barrier((rest_below, rest_above, bins, px))
    far_below = moved(jnp.concatenate([pair_below[:1], rest_below[:3]], 0), "x", 4, 1)
    far_above = moved(jnp.concatenate([pair_above[1:], rest_above[3:]], 0), "x", 4, -1)
    columns = (
        jnp.concatenate([pair_below, rest_below, pair_above, rest_above], 0),
        jnp.concatenate([far_below[:1], far_above[:1], far_below[1:], far_above[1:]], 0),
        jnp.concatenate([pair, rest], 0),
    )
    acc = shape((64, PROBES, TILE), f32)
    block = shape((8, 256, TILE), bf16)

    def pairs(part, totals=None):
        tiles = PARTS[part] * 64
        outs = (acc,) + (block,) * (PARTS[part] + (part == 2))
        operands = (place, counts, bins, row_all, px, py, columns[part]) + (() if part == 0 else (totals,))
        return pl.pallas_call(
            functools.partial(part_kernel, part),
            out_shape=outs,
            in_specs=[SMEM] * 3 + [VMEM] * (len(operands) - 3),
            out_specs=(VMEM,) * len(outs),
            scratch_shapes=[pltpu.VMEM((tiles, 8, TILE), f32)] * 2 + [pltpu.VMEM((tiles, PROBES, TILE), f32)],
            input_output_aliases={} if part == 0 else {7: 0},
            compiler_params=PARAMS,
            name="pairs",
        )(*operands)

    totals, for_below, for_above = pairs(0)
    below, above = moved(for_below, "x", 4, -1), moved(for_above, "x", 4, 1)
    totals, for_far = pairs(1, totals)
    far = moved(for_far, "x", 4, 2)
    totals, row_sum, own = pairs(2, totals)
    sums = pl.pallas_call(
        add_kernel,
        out_shape=block,
        in_specs=[VMEM] * 4,
        out_specs=VMEM,
        compiler_params=PARAMS,
        name="add",
    )(own, below, far, above)
    col_parts = lax.all_to_all(sums, "z", 0, 0)
    half = (row_sum[:4].astype(f32) + swap(row_sum[4:]).astype(f32)).astype(bf16)
    row_parts = [half[0]] + [
        lax.ppermute(half[k], "y", [(i, (i - k) % 4) for i in range(4)]) for k in range(1, 4)
    ]
    row_parts = jnp.stack(row_parts)
    image, gram = pl.pallas_call(
        gram_kernel,
        out_shape=(shape((PROBES, own_points), f32), shape((40, TILE), f32)),
        in_specs=[VMEM] * 5,
        out_specs=(VMEM, VMEM),
        compiler_params=PARAMS,
        name="gram",
    )(direction, residual, own_product, row_parts, col_parts)
    gram = gram + swap(gram)
    gram = sum(shifts(gram, "y", 4), gram)
    gram = sum(shifts(gram, "x", 4), gram)
    gram = gram + lax.ppermute(gram, "z", [(i, (i + 4) % 8) for i in range(8)])
    gram = sum(shifts(gram, "z", 8)[:3], gram)
    return pl.pallas_call(
        solve_kernel,
        out_shape=(shape((PROBES, own_points), f32),) * 3,
        in_specs=[VMEM] * 5,
        out_specs=(VMEM,) * 3,
        compiler_params=PARAMS,
        name="solve",
    )(gram, solution_field, residual, direction, image)


def solution(mesh):
    fine = Mesh(np.asarray(mesh.devices).reshape(8, 4, 4, 2), ("z", "x", "y", "core"))
    points = P(None, ("z", "x", "y", "core"))
    return jax.shard_map(
        on_device,
        mesh=fine,
        in_specs=(points,) * 5 + (P(("z", "x", "y", "core")),),
        out_specs=(points,) * 3,
        check_vma=False,
    )
```

```python
import functools

import jax
import jax.numpy as jnp
import numpy as np
from jax import lax
from jax.experimental import pallas as pl
from jax.experimental.pallas import tpu as pltpu
from jax.sharding import Mesh
from jax.sharding import PartitionSpec as P

TILE = 128
PROBES = 32
UNROLL = 32
TAIL = 8
PARTS = (2, 1, 1)
LIST = 1536 + UNROLL
NUGGET = 2.0
KERNEL_SCALE = 0.1
HIGHEST = lax.Precision.HIGHEST
f32, bf16 = jnp.float32, jnp.bfloat16
VMEM = pl.BlockSpec(memory_space=pltpu.VMEM)
SMEM = pl.BlockSpec(memory_space=pltpu.SMEM)
NT = (((1,), (1,)), ((), ()))
NN = (((1,), (0,)), ((), ()))
TN = (((0,), (0,)), ((), ()))
PARAMS = pltpu.CompilerParams(vmem_limit_bytes=16 * 2**20)
SMALL = pltpu.CompilerParams(vmem_limit_bytes=4 * 2**20)


def pack_kernel(direction_ref, positions_ref, packed_ref):
    for t in range(8):
        packed_ref[t * 32 : (t + 1) * 32, :] = direction_ref[:, t * TILE : (t + 1) * TILE].astype(bf16)
    where = positions_ref[...].astype(f32)
    rows = [where[d : d + 1, t * TILE : (t + 1) * TILE] for d in range(2) for t in range(8)]
    packed_ref[256:272, :] = jnp.concatenate(rows, 0).astype(bf16)


def radial(square):
    distance = pl.reciprocal(lax.rsqrt(square), approx=True)
    remain = jnp.maximum(1.0 - distance, 0.0)
    remain2 = remain * remain
    return ((remain2 * remain2) * (1.25 - remain)).astype(bf16)


def bin_kernel(live_ref, entries_ref, after_ref, bins_ref, count_ref):
    live = live_ref[0]

    def put(e, entry, ends):
        first, second = ends
        bins_ref[first] = entry
        bins_ref[LIST + second] = entry
        bins_ref[2 * LIST + e - first - second] = entry
        return first + ((entry >> 16) & 1), second + ((entry >> 17) & 1)

    def step(i, ends):
        entries = [entries_ref[i * 16 + u] for u in range(16)]
        for u in range(16):
            ends = put(i * 16 + u, entries[u], ends)
        return ends

    groups = live >> 4
    ends = lax.fori_loop(0, groups, step, (jnp.int32(0), jnp.int32(0)))
    first, second = lax.fori_loop(groups * 16, live, lambda e, ends: put(e, entries_ref[e], ends), ends)
    for part, end in enumerate((first, second, live - first - second)):
        count_ref[part] = end
        for j in range(TAIL):
            bins_ref[part * LIST + end + j] = 0


def spread(strip, t):
    return jnp.broadcast_to(strip[:, t : t + 1], (TILE, TILE))


def row_kernel(own_ref, near_ref, px, py, own_out):
    def row_prepare(r, carry):
        strip = near_ref[r, 256:272, :].astype(f32).T
        for t in range(8):
            px[r * 8 + t] = spread(strip, t)
            py[r * 8 + t] = spread(strip, 8 + t)
        return carry

    lax.fori_loop(0, 8, row_prepare, 0)
    where = own_ref[256:272, :].astype(f32)
    strip = where.T
    for t in range(8):
        dx = spread(strip, t) - where[t : t + 1]
        dy = spread(strip, 8 + t) - where[8 + t : 9 + t]
        block = radial(dx * dx + dy * dy)
        own_out[:, t * TILE : (t + 1) * TILE] = KERNEL_SCALE * lax.dot_general(
            own_ref[t * 32 : (t + 1) * 32, :], block, NT, preferred_element_type=f32
        )


def z_slot(distance):
    low, high = distance & 3, distance >> 2
    return (low << 1) + (high ^ (low & (low >> 1)))


def part_kernel(part, place_ref, count_ref, bins_ref, near_ref, px, py, col_ref, *refs):
    if part == 0:
        row_acc, *col_out, qx, qy, col_acc = refs
        row_acc[...] = jnp.zeros_like(row_acc)
    elif part == 1:
        before, row_acc, *col_out, qx, qy, col_acc = refs
        row_acc[...] = before[...]
    else:
        before, row_acc, row_out, *col_out, qx, qy, col_acc = refs
        row_acc[...] = before[...]
    z_own = place_ref[0]
    live = count_ref[part]
    col_acc[...] = jnp.zeros_like(col_acc)

    def col_prepare(r, carry):
        where = col_ref[r, 256:272, :].astype(f32)
        for t in range(8):
            qx[r * 8 + t] = jnp.broadcast_to(where[t : t + 1], (8, TILE))
            qy[r * 8 + t] = jnp.broadcast_to(where[8 + t : 9 + t], (8, TILE))
        return carry

    lax.fori_loop(0, 8 * PARTS[part], col_prepare, 0)

    def several(start, size, masked):
        results = []
        for u in range(size):
            e = start + u
            entry = bins_ref[part * LIST + e]
            a, b = entry & 255, (entry >> 8) & 255
            near = near_ref[a >> 3, pl.ds(pl.multiple_of((a & 7) * 32, 32), 32), :]
            far = col_ref[b >> 3, pl.ds(pl.multiple_of((b & 7) * 32, 32), 32), :]
            if masked:
                keep = jnp.where(e < live, 1.0, 0.0).astype(bf16)
                near, far = near * keep, far * keep
            dx = px[a].reshape(16, 8, TILE) - qx[b][None]
            dy = py[a].reshape(16, 8, TILE) - qy[b][None]
            block = radial((dx * dx + dy * dy).reshape(TILE, TILE))
            forward = lax.dot_general(far, block, NT, preferred_element_type=f32)
            backward = lax.dot_general(near, block, NN, preferred_element_type=f32)
            results.append((a, b, forward, backward))
        for a, b, forward, backward in results:
            row_acc[a] += forward
            col_acc[b] += backward

    whole = live // UNROLL

    def body(i, carry):
        several(i * UNROLL, UNROLL, False)
        return carry

    def tail(i, carry):
        several(whole * UNROLL + i * TAIL, TAIL, True)
        return carry

    lax.fori_loop(0, whole, body, 0)
    lax.fori_loop(0, (live - whole * UNROLL + TAIL - 1) // TAIL, tail, 0)

    def finish(z, carry):
        for k in range(PARTS[part]):
            for t in range(8):
                total = KERNEL_SCALE * col_acc[k * 64 + z_slot(z) * 8 + t]
                col_out[k][(z_own - z) & 7, t * 32 : (t + 1) * 32, :] = total.astype(bf16)
        return carry

    lax.fori_loop(0, 8, finish, 0)
    if part == 2:

        def finish_row(r, carry):
            for t in range(8):
                row_out[r, t * 32 : (t + 1) * 32, :] = (KERNEL_SCALE * row_acc[r * 8 + t]).astype(bf16)
            return carry

        lax.fori_loop(0, 8, finish_row, 0)


def add_kernel(own, below, far, above, out):
    for z in range(8):
        total = (own[z].astype(f32) + below[z].astype(f32)) + (far[z].astype(f32) + above[z].astype(f32))
        out[z] = total.astype(bf16)


def dot32(former, latter, dims):
    return lax.dot_general(former, latter, dims, precision=HIGHEST, preferred_element_type=f32)


def gram_kernel(direction_ref, residual_ref, own_ref, row_ref, col_ref, image_ref, gram_ref):
    for t in range(8):
        here = slice(t * 32, (t + 1) * 32)
        lanes = slice(t * TILE, (t + 1) * TILE)
        total = NUGGET * direction_ref[:, lanes] + own_ref[:, lanes]
        for part in range(row_ref.shape[0]):
            total = total + row_ref[part, here, :].astype(f32)
        for part in range(col_ref.shape[0]):
            total = total + col_ref[part, here, :].astype(f32)
        image_ref[:, lanes] = total
    direction, residual, image = direction_ref[...], residual_ref[...], image_ref[...]
    gram_ref[0:32, 0:32] = dot32(direction, image, NT)
    gram_ref[0:32, 32:64] = dot32(direction, residual, NT)
    gram_ref[0:32, 64:96] = dot32(residual, residual, NT)
    gram_ref[0:32, 96:128] = dot32(residual, image, NT)
    square = dot32(image, image, NT)
    for t in range(4):
        gram_ref[32:40, t * 32 : (t + 1) * 32] = square[t * 8 : (t + 1) * 8]


def solve_kernel(gram_ref, solution_ref, residual_ref, direction_ref, image_ref, solution_out, residual_out, direction_out):
    gram = gram_ref[...]
    curvature, crossing = gram[0:32, 0:32], gram[0:32, 32:64]
    norm_old, mixed = gram[0:32, 64:96], gram[0:32, 96:128]
    square = jnp.concatenate([gram[32:40, t * 32 : (t + 1) * 32] for t in range(4)], 0)
    row = lax.broadcasted_iota(jnp.int32, (32, 64), 0)
    lane = lax.broadcasted_iota(jnp.int32, (32, 64), 1)
    unit = jnp.where(row[:, :32] == lane[:, :32], 1.0, 0.0).astype(f32)
    first = jnp.concatenate([0.5 * (curvature + curvature.T), crossing], 1)
    second = jnp.concatenate([0.5 * (norm_old + norm_old.T), unit], 1)

    def eliminate(table, k):
        pivot_row = table[k : k + 1, :] / table[k : k + 1, k : k + 1]
        return jnp.where(row == k, pivot_row, table - table[:, k : k + 1] * pivot_row)

    for k in range(32):
        first, second = eliminate(first, k), eliminate(second, k)
    alpha, inverse = first[:, 32:64], second[:, 32:64]
    cross = dot32(mixed, alpha, NN)
    norm_new = 0.5 * (norm_old + norm_old.T) - cross - cross.T + dot32(alpha, dot32(square, alpha, NN), TN)
    beta = dot32(inverse, norm_new, NN)
    direction = direction_ref[...]
    residual_next = residual_ref[...] - dot32(alpha, image_ref[...], TN)
    residual_out[...] = residual_next
    solution_out[...] = solution_ref[...] + dot32(alpha, direction, TN)
    direction_out[...] = residual_next + dot32(beta, direction, TN)


def shifts(value, axis, size):
    return [lax.ppermute(value, axis, [(i, (i + k) % size) for i in range(size)]) for k in range(1, size)]


def swap(value):
    return lax.ppermute(value, "core", [(0, 1), (1, 0)])


def on_device(solution_field, residual, direction, positions, tile_pairs, pair_count):
    shape = jax.ShapeDtypeStruct
    own_points = direction.shape[1]
    packed = pl.pallas_call(
        pack_kernel, out_shape=shape((272, TILE), bf16), in_specs=[VMEM] * 2, out_specs=VMEM, compiler_params=SMALL, name="pack"
    )(direction, positions)
    def moved(value, axis, size, shift):
        return lax.ppermute(value, axis, [(i, (i + shift) % size) for i in range(size)])

    row_half = jnp.stack([packed] + shifts(packed, "y", 4))
    pair = jnp.stack([packed, moved(packed, "z", 8, 4)])
    one, two, back = [moved(pair, "z", 8, shift) for shift in (1, 2, -1)]
    pair_below, pair_above = moved(pair, "x", 4, 1), moved(pair, "x", 4, -1)
    rest = jnp.concatenate([one, two, back], 0)
    row_half, rest = lax.optimization_barrier((row_half, rest))
    rest_below, rest_above = moved(rest, "x", 4, 1), moved(rest, "x", 4, -1)
    row_all = jnp.concatenate([row_half, swap(row_half)], 0)
    x_own, y_own, z_own, core_own = [lax.axis_index(name).astype(jnp.int32) for name in ("x", "y", "z", "core")]
    place = z_own.reshape(1)
    a, b = tile_pairs[0], tile_pairs[1]
    near_slot = ((y_own - (a >> 4)) & 3) + ((((a >> 3) & 1) ^ core_own) << 2)
    x_far = (x_own - (b >> 3)) & 3
    far_slot = z_slot((z_own - (b >> 5)) & 7) + jnp.where(x_far == 3, 8, 0)
    entries = (near_slot << 3) + (a & 7) + (far_slot << 11) + ((b & 7) << 8)
    entries = entries + ((x_far & 1) << 16) + jnp.where(x_far == 2, 1 << 17, 0)
    bins, counts = pl.pallas_call(
        bin_kernel,
        out_shape=(shape((3 * LIST,), jnp.int32), shape((3,), jnp.int32)),
        in_specs=[SMEM, SMEM, VMEM],
        out_specs=(SMEM, SMEM),
        compiler_params=SMALL,
        name="bins",
    )(pair_count, entries, pair_above[0, :16])
    spread_shape = shape((64, TILE, TILE), f32)
    px, py, own_product = pl.pallas_call(
        row_kernel,
        out_shape=(spread_shape, spread_shape, shape((PROBES, own_points), f32)),
        in_specs=[VMEM] * 2,
        out_specs=(VMEM,) * 3,
        compiler_params=PARAMS,
        name="rows",
    )(packed, row_all)
    rest_below, rest_above, bins, px = lax.optimization_barrier((rest_below, rest_above, bins, px))
    far_below = moved(jnp.concatenate([pair_below[:1], rest_below[:3]], 0), "x", 4, 1)
    far_above = moved(jnp.concatenate([pair_above[1:], rest_above[3:]], 0), "x", 4, -1)
    columns = (
        jnp.concatenate([pair_below, rest_below, pair_above, rest_above], 0),
        jnp.concatenate([far_below[:1], far_above[:1], far_below[1:], far_above[1:]], 0),
        jnp.concatenate([pair, rest], 0),
    )
    acc = shape((64, PROBES, TILE), f32)
    block = shape((8, 256, TILE), bf16)

    def pairs(part, totals=None):
        tiles = PARTS[part] * 64
        outs = (acc,) + (block,) * (PARTS[part] + (part == 2))
        operands = (place, counts, bins, row_all, px, py, columns[part]) + (() if part == 0 else (totals,))
        return pl.pallas_call(
            functools.partial(part_kernel, part),
            out_shape=outs,
            in_specs=[SMEM] * 3 + [VMEM] * (len(operands) - 3),
            out_specs=(VMEM,) * len(outs),
            scratch_shapes=[pltpu.VMEM((tiles, 8, TILE), f32)] * 2 + [pltpu.VMEM((tiles, PROBES, TILE), f32)],
            input_output_aliases={} if part == 0 else {7: 0},
            compiler_params=PARAMS,
            name="pairs",
        )(*operands)

    totals, for_below, for_above = pairs(0)
    below, above = moved(for_below, "x", 4, -1), moved(for_above, "x", 4, 1)
    totals, for_far = pairs(1, totals)
    far = moved(for_far, "x", 4, 2)
    totals, row_sum, own = pairs(2, totals)
    sums = pl.pallas_call(
        add_kernel,
        out_shape=block,
        in_specs=[VMEM] * 4,
        out_specs=VMEM,
        compiler_params=PARAMS,
        name="add",
    )(own, below, far, above)
    col_parts = lax.all_to_all(sums, "z", 0, 0)
    half = (row_sum[:4].astype(f32) + swap(row_sum[4:]).astype(f32)).astype(bf16)
    row_parts = [half[0]] + [
        lax.ppermute(half[k], "y", [(i, (i - k) % 4) for i in range(4)]) for k in range(1, 4)
    ]
    row_parts = jnp.stack(row_parts)
    image, gram = pl.pallas_call(
        gram_kernel,
        out_shape=(shape((PROBES, own_points), f32), shape((40, TILE), f32)),
        in_specs=[VMEM] * 5,
        out_specs=(VMEM, VMEM),
        compiler_params=PARAMS,
        name="gram",
    )(direction, residual, own_product, row_parts, col_parts)
    gram = gram + swap(gram)
    gram = sum(shifts(gram, "y", 4), gram)
    gram = sum(shifts(gram, "x", 4), gram)
    gram = gram + moved(gram, "z", 8, 1)
    gram = sum([moved(gram, "z", 8, shift) for shift in (4, 2, -2)], gram)
    return pl.pallas_call(
        solve_kernel,
        out_shape=(shape((PROBES, own_points), f32),) * 3,
        in_specs=[VMEM] * 5,
        out_specs=(VMEM,) * 3,
        compiler_params=PARAMS,
        name="solve",
    )(gram, solution_field, residual, direction, image)


def solution(mesh):
    fine = Mesh(np.asarray(mesh.devices).reshape(8, 4, 4, 2), ("z", "x", "y", "core"))
    points = P(None, ("z", "x", "y", "core"))
    return jax.shard_map(
        on_device,
        mesh=fine,
        in_specs=(points,) * 5 + (P(("z", "x", "y", "core")),),
        out_specs=(points,) * 3,
        check_vma=False,
    )
```

```python
import functools

import jax
import jax.numpy as jnp
import numpy as np
from jax import lax
from jax.experimental import pallas as pl
from jax.experimental.pallas import tpu as pltpu
from jax.sharding import Mesh
from jax.sharding import PartitionSpec as P

TILE = 128
PROBES = 32
UNROLL = 32
TAIL = 8
PARTS = (2, 1, 1)
LIST = 1536 + UNROLL
NUGGET = 2.0
KERNEL_SCALE = 0.1
HIGHEST = lax.Precision.HIGHEST
f32, bf16 = jnp.float32, jnp.bfloat16
VMEM = pl.BlockSpec(memory_space=pltpu.VMEM)
SMEM = pl.BlockSpec(memory_space=pltpu.SMEM)
NT = (((1,), (1,)), ((), ()))
NN = (((1,), (0,)), ((), ()))
TN = (((0,), (0,)), ((), ()))
PARAMS = pltpu.CompilerParams(vmem_limit_bytes=16 * 2**20)
SMALL = pltpu.CompilerParams(vmem_limit_bytes=4 * 2**20)


def pack_kernel(direction_ref, positions_ref, packed_ref):
    for t in range(8):
        packed_ref[t * 32 : (t + 1) * 32, :] = direction_ref[:, t * TILE : (t + 1) * TILE].astype(bf16)
    where = positions_ref[...].astype(f32)
    rows = [where[d : d + 1, t * TILE : (t + 1) * TILE] for d in range(2) for t in range(8)]
    packed_ref[256:272, :] = jnp.concatenate(rows, 0).astype(bf16)


def radial(square):
    distance = pl.reciprocal(lax.rsqrt(square), approx=True)
    remain = jnp.maximum(1.0 - distance, 0.0)
    remain2 = remain * remain
    return ((remain2 * remain2) * (1.25 - remain)).astype(bf16)


def bin_kernel(live_ref, entries_ref, count_ref, after_ref, bins_ref):
    live = live_ref[0]

    def step(i, carry):
        entries = [entries_ref[i * 16 + u] for u in range(16)]
        for entry in entries:
            bins_ref[entry >> 16] = entry
        return carry

    def last(e, carry):
        entry = entries_ref[e]
        bins_ref[entry >> 16] = entry
        return carry

    groups = live >> 4
    lax.fori_loop(0, groups, step, 0)
    lax.fori_loop(groups * 16, live, last, 0)
    for part in range(3):
        for j in range(TAIL):
            bins_ref[part * LIST + count_ref[part] + j] = 0


def spread(strip, t):
    return jnp.broadcast_to(strip[:, t : t + 1], (TILE, TILE))


def row_kernel(own_ref, near_ref, px, py, own_out):
    def row_prepare(r, carry):
        strip = near_ref[r, 256:272, :].astype(f32).T
        for t in range(8):
            px[r * 8 + t] = spread(strip, t)
            py[r * 8 + t] = spread(strip, 8 + t)
        return carry

    lax.fori_loop(0, 8, row_prepare, 0)
    where = own_ref[256:272, :].astype(f32)
    strip = where.T
    for t in range(8):
        dx = spread(strip, t) - where[t : t + 1]
        dy = spread(strip, 8 + t) - where[8 + t : 9 + t]
        block = radial(dx * dx + dy * dy)
        own_out[:, t * TILE : (t + 1) * TILE] = KERNEL_SCALE * lax.dot_general(
            own_ref[t * 32 : (t + 1) * 32, :], block, NT, preferred_element_type=f32
        )


def z_slot(distance):
    low, high = distance & 3, distance >> 2
    return (low << 1) + (high ^ (low & (low >> 1)))


def part_kernel(part, place_ref, count_ref, bins_ref, near_ref, px, py, col_ref, *refs):
    if part == 0:
        row_acc, *col_out, qx, qy, col_acc = refs
        row_acc[...] = jnp.zeros_like(row_acc)
    elif part == 1:
        before, row_acc, *col_out, qx, qy, col_acc = refs
        row_acc[...] = before[...]
    else:
        before, row_acc, row_out, *col_out, qx, qy, col_acc = refs
        row_acc[...] = before[...]
    z_own = place_ref[0]
    live = count_ref[part]
    col_acc[...] = jnp.zeros_like(col_acc)

    def col_prepare(r, carry):
        where = col_ref[r, 256:272, :].astype(f32)
        for t in range(8):
            qx[r * 8 + t] = jnp.broadcast_to(where[t : t + 1], (8, TILE))
            qy[r * 8 + t] = jnp.broadcast_to(where[8 + t : 9 + t], (8, TILE))
        return carry

    lax.fori_loop(0, 8 * PARTS[part], col_prepare, 0)

    def several(start, size, masked):
        results = []
        for u in range(size):
            e = start + u
            entry = bins_ref[part * LIST + e]
            a, b = entry & 255, (entry >> 8) & 255
            near = near_ref[a >> 3, pl.ds(pl.multiple_of((a & 7) * 32, 32), 32), :]
            far = col_ref[b >> 3, pl.ds(pl.multiple_of((b & 7) * 32, 32), 32), :]
            if masked:
                keep = jnp.where(e < live, 1.0, 0.0).astype(bf16)
                near, far = near * keep, far * keep
            dx = px[a].reshape(16, 8, TILE) - qx[b][None]
            dy = py[a].reshape(16, 8, TILE) - qy[b][None]
            block = radial((dx * dx + dy * dy).reshape(TILE, TILE))
            forward = lax.dot_general(far, block, NT, preferred_element_type=f32)
            backward = lax.dot_general(near, block, NN, preferred_element_type=f32)
            results.append((a, b, forward, backward))
        for a, b, forward, backward in results:
            row_acc[a] += forward
            col_acc[b] += backward

    whole = live // UNROLL

    def body(i, carry):
        several(i * UNROLL, UNROLL, False)
        return carry

    def tail(i, carry):
        several(whole * UNROLL + i * TAIL, TAIL, True)
        return carry

    lax.fori_loop(0, whole, body, 0)
    lax.fori_loop(0, (live - whole * UNROLL + TAIL - 1) // TAIL, tail, 0)

    def finish(z, carry):
        for k in range(PARTS[part]):
            for t in range(8):
                total = KERNEL_SCALE * col_acc[k * 64 + z_slot(z) * 8 + t]
                col_out[k][(z_own - z) & 7, t * 32 : (t + 1) * 32, :] = total.astype(bf16)
        return carry

    lax.fori_loop(0, 8, finish, 0)
    if part == 2:

        def finish_row(r, carry):
            for t in range(8):
                row_out[r, t * 32 : (t + 1) * 32, :] = (KERNEL_SCALE * row_acc[r * 8 + t]).astype(bf16)
            return carry

        lax.fori_loop(0, 8, finish_row, 0)


def add_kernel(own, below, far, above, out):
    for z in range(8):
        total = (own[z].astype(f32) + below[z].astype(f32)) + (far[z].astype(f32) + above[z].astype(f32))
        out[z] = total.astype(bf16)


def dot32(former, latter, dims):
    return lax.dot_general(former, latter, dims, precision=HIGHEST, preferred_element_type=f32)


def gram_kernel(direction_ref, residual_ref, own_ref, row_ref, col_ref, image_ref, gram_ref):
    for t in range(8):
        here = slice(t * 32, (t + 1) * 32)
        lanes = slice(t * TILE, (t + 1) * TILE)
        total = NUGGET * direction_ref[:, lanes] + own_ref[:, lanes]
        for part in range(row_ref.shape[0]):
            total = total + row_ref[part, here, :].astype(f32)
        for part in range(col_ref.shape[0]):
            total = total + col_ref[part, here, :].astype(f32)
        image_ref[:, lanes] = total
    direction, residual, image = direction_ref[...], residual_ref[...], image_ref[...]
    gram_ref[0:32, 0:32] = dot32(direction, image, NT)
    gram_ref[0:32, 32:64] = dot32(direction, residual, NT)
    gram_ref[0:32, 64:96] = dot32(residual, residual, NT)
    gram_ref[0:32, 96:128] = dot32(residual, image, NT)
    square = dot32(image, image, NT)
    for t in range(4):
        gram_ref[32:40, t * 32 : (t + 1) * 32] = square[t * 8 : (t + 1) * 8]


def solve_kernel(gram_ref, solution_ref, residual_ref, direction_ref, image_ref, solution_out, residual_out, direction_out):
    gram = gram_ref[...]
    curvature, crossing = gram[0:32, 0:32], gram[0:32, 32:64]
    norm_old, mixed = gram[0:32, 64:96], gram[0:32, 96:128]
    square = jnp.concatenate([gram[32:40, t * 32 : (t + 1) * 32] for t in range(4)], 0)
    row = lax.broadcasted_iota(jnp.int32, (32, 64), 0)
    lane = lax.broadcasted_iota(jnp.int32, (32, 64), 1)
    unit = jnp.where(row[:, :32] == lane[:, :32], 1.0, 0.0).astype(f32)
    first = jnp.concatenate([0.5 * (curvature + curvature.T), crossing], 1)
    second = jnp.concatenate([0.5 * (norm_old + norm_old.T), unit], 1)

    def eliminate(table, k):
        pivot_row = table[k : k + 1, :] / table[k : k + 1, k : k + 1]
        return jnp.where(row == k, pivot_row, table - table[:, k : k + 1] * pivot_row)

    for k in range(32):
        first, second = eliminate(first, k), eliminate(second, k)
    alpha, inverse = first[:, 32:64], second[:, 32:64]
    cross = dot32(mixed, alpha, NN)
    norm_new = 0.5 * (norm_old + norm_old.T) - cross - cross.T + dot32(alpha, dot32(square, alpha, NN), TN)
    beta = dot32(inverse, norm_new, NN)
    direction = direction_ref[...]
    residual_next = residual_ref[...] - dot32(alpha, image_ref[...], TN)
    residual_out[...] = residual_next
    solution_out[...] = solution_ref[...] + dot32(alpha, direction, TN)
    direction_out[...] = residual_next + dot32(beta, direction, TN)


def shifts(value, axis, size):
    return [lax.ppermute(value, axis, [(i, (i + k) % size) for i in range(size)]) for k in range(1, size)]


def swap(value):
    return lax.ppermute(value, "core", [(0, 1), (1, 0)])


def on_device(solution_field, residual, direction, positions, tile_pairs, pair_count):
    shape = jax.ShapeDtypeStruct
    own_points = direction.shape[1]
    packed = pl.pallas_call(
        pack_kernel, out_shape=shape((272, TILE), bf16), in_specs=[VMEM] * 2, out_specs=VMEM, compiler_params=SMALL, name="pack"
    )(direction, positions)
    def moved(value, axis, size, shift):
        return lax.ppermute(value, axis, [(i, (i + shift) % size) for i in range(size)])

    row_half = jnp.stack([packed] + shifts(packed, "y", 4))
    pair = jnp.stack([packed, moved(packed, "z", 8, 4)])
    one, two, back = [moved(pair, "z", 8, shift) for shift in (1, 2, -1)]
    pair_below, pair_above = moved(pair, "x", 4, 1), moved(pair, "x", 4, -1)
    rest = jnp.concatenate([one, two, back], 0)
    row_half, rest = lax.optimization_barrier((row_half, rest))
    rest_below, rest_above = moved(rest, "x", 4, 1), moved(rest, "x", 4, -1)
    row_all = jnp.concatenate([row_half, swap(row_half)], 0)
    x_own, y_own, z_own, core_own = [lax.axis_index(name).astype(jnp.int32) for name in ("x", "y", "z", "core")]
    place = z_own.reshape(1)
    tile_pairs, counted, pair_above, row_half = lax.optimization_barrier((tile_pairs, pair_count, pair_above, row_half))
    a, b = tile_pairs[0], tile_pairs[1]
    near_slot = ((y_own - (a >> 4)) & 3) + ((((a >> 3) & 1) ^ core_own) << 2)
    x_far = (x_own - (b >> 3)) & 3
    far_slot = z_slot((z_own - (b >> 5)) & 7) + jnp.where(x_far == 3, 8, 0)
    entries = (near_slot << 3) + (a & 7) + (far_slot << 11) + ((b & 7) << 8)
    part = jnp.where(x_far == 2, 1, jnp.where(x_far == 0, 2, 0))
    part = jnp.where(jnp.arange(part.shape[0], dtype=jnp.int32) < counted[0], part, 3).reshape(-1, TILE)
    hot = (part[None] == jnp.arange(3, dtype=jnp.int32)[:, None, None]).astype(bf16)
    ahead = jnp.triu(jnp.ones((TILE, TILE), bf16), 1)
    rows = hot.shape[1]
    ahead_row = jnp.einsum("prl,lm->prm", hot, ahead, preferred_element_type=f32)
    row_count = jnp.sum(hot.astype(f32), 2)
    ahead_rows = jnp.sum(row_count[:, :, None] * jnp.triu(jnp.ones((rows, rows), f32), 1)[None], 1)
    spot = ahead_row + ahead_rows[:, :, None] + (jnp.arange(3, dtype=jnp.int32) * LIST).astype(f32)[:, None, None]
    spot = jnp.sum(hot.astype(f32) * spot, 0).astype(jnp.int32).reshape(-1)
    entries = entries + (spot << 16)
    counts = jnp.sum(row_count, 1).astype(jnp.int32)
    bins = pl.pallas_call(
        bin_kernel,
        out_shape=shape((3 * LIST,), jnp.int32),
        in_specs=[SMEM, SMEM, SMEM, VMEM],
        out_specs=SMEM,
        compiler_params=SMALL,
        name="bins",
    )(pair_count, entries, counts, pair_above[0, :16])
    spread_shape = shape((64, TILE, TILE), f32)
    px, py, own_product = pl.pallas_call(
        row_kernel,
        out_shape=(spread_shape, spread_shape, shape((PROBES, own_points), f32)),
        in_specs=[VMEM] * 2,
        out_specs=(VMEM,) * 3,
        compiler_params=PARAMS,
        name="rows",
    )(packed, row_all)
    rest_below, rest_above, bins, px = lax.optimization_barrier((rest_below, rest_above, bins, px))
    far_below = moved(jnp.concatenate([pair_below[:1], rest_below[:3]], 0), "x", 4, 1)
    far_above = moved(jnp.concatenate([pair_above[1:], rest_above[3:]], 0), "x", 4, -1)
    columns = (
        jnp.concatenate([pair_below, rest_below, pair_above, rest_above], 0),
        jnp.concatenate([far_below[:1], far_above[:1], far_below[1:], far_above[1:]], 0),
        jnp.concatenate([pair, rest], 0),
    )
    acc = shape((64, PROBES, TILE), f32)
    block = shape((8, 256, TILE), bf16)

    def pairs(part, totals=None):
        tiles = PARTS[part] * 64
        outs = (acc,) + (block,) * (PARTS[part] + (part == 2))
        operands = (place, counts, bins, row_all, px, py, columns[part]) + (() if part == 0 else (totals,))
        return pl.pallas_call(
            functools.partial(part_kernel, part),
            out_shape=outs,
            in_specs=[SMEM] * 3 + [VMEM] * (len(operands) - 3),
            out_specs=(VMEM,) * len(outs),
            scratch_shapes=[pltpu.VMEM((tiles, 8, TILE), f32)] * 2 + [pltpu.VMEM((tiles, PROBES, TILE), f32)],
            input_output_aliases={} if part == 0 else {7: 0},
            compiler_params=PARAMS,
            name="pairs",
        )(*operands)

    totals, for_below, for_above = pairs(0)
    below, above = moved(for_below, "x", 4, -1), moved(for_above, "x", 4, 1)
    totals, for_far = pairs(1, totals)
    far = moved(for_far, "x", 4, 2)
    totals, row_sum, own = pairs(2, totals)
    sums = pl.pallas_call(
        add_kernel,
        out_shape=block,
        in_specs=[VMEM] * 4,
        out_specs=VMEM,
        compiler_params=PARAMS,
        name="add",
    )(own, below, far, above)
    col_parts = lax.all_to_all(sums, "z", 0, 0)
    half = (row_sum[:4].astype(f32) + swap(row_sum[4:]).astype(f32)).astype(bf16)
    row_parts = [half[0]] + [
        lax.ppermute(half[k], "y", [(i, (i - k) % 4) for i in range(4)]) for k in range(1, 4)
    ]
    row_parts = jnp.stack(row_parts)
    image, gram = pl.pallas_call(
        gram_kernel,
        out_shape=(shape((PROBES, own_points), f32), shape((40, TILE), f32)),
        in_specs=[VMEM] * 5,
        out_specs=(VMEM, VMEM),
        compiler_params=PARAMS,
        name="gram",
    )(direction, residual, own_product, row_parts, col_parts)
    gram = gram + swap(gram)
    gram = sum(shifts(gram, "y", 4), gram)
    gram = sum(shifts(gram, "x", 4), gram)
    gram = gram + lax.ppermute(gram, "z", [(i, (i + 4) % 8) for i in range(8)])
    gram = sum(shifts(gram, "z", 8)[:3], gram)
    return pl.pallas_call(
        solve_kernel,
        out_shape=(shape((PROBES, own_points), f32),) * 3,
        in_specs=[VMEM] * 5,
        out_specs=(VMEM,) * 3,
        compiler_params=PARAMS,
        name="solve",
    )(gram, solution_field, residual, direction, image)


def solution(mesh):
    fine = Mesh(np.asarray(mesh.devices).reshape(8, 4, 4, 2), ("z", "x", "y", "core"))
    points = P(None, ("z", "x", "y", "core"))
    return jax.shard_map(
        on_device,
        mesh=fine,
        in_specs=(points,) * 5 + (P(("z", "x", "y", "core")),),
        out_specs=(points,) * 3,
        check_vma=False,
    )
```

```python
import functools

import jax
import jax.numpy as jnp
import numpy as np
from jax import lax
from jax.experimental import pallas as pl
from jax.experimental.pallas import tpu as pltpu
from jax.sharding import Mesh
from jax.sharding import PartitionSpec as P

TILE = 128
PROBES = 32
UNROLL = 32
TAIL = 8
PARTS = (2, 1, 1)
LIST = 1536 + UNROLL
NUGGET = 2.0
KERNEL_SCALE = 0.1
HIGHEST = lax.Precision.HIGHEST
f32, bf16 = jnp.float32, jnp.bfloat16
VMEM = pl.BlockSpec(memory_space=pltpu.VMEM)
SMEM = pl.BlockSpec(memory_space=pltpu.SMEM)
NT = (((1,), (1,)), ((), ()))
NN = (((1,), (0,)), ((), ()))
TN = (((0,), (0,)), ((), ()))
PARAMS = pltpu.CompilerParams(vmem_limit_bytes=16 * 2**20)
SMALL = pltpu.CompilerParams(vmem_limit_bytes=4 * 2**20)


def pack_kernel(direction_ref, positions_ref, packed_ref):
    for t in range(8):
        packed_ref[t * 32 : (t + 1) * 32, :] = direction_ref[:, t * TILE : (t + 1) * TILE].astype(bf16)
    where = positions_ref[...].astype(f32)
    rows = [where[d : d + 1, t * TILE : (t + 1) * TILE] for d in range(2) for t in range(8)]
    packed_ref[256:272, :] = jnp.concatenate(rows, 0).astype(bf16)


def radial(square):
    distance = pl.reciprocal(lax.rsqrt(square), approx=True)
    remain = jnp.maximum(1.0 - distance, 0.0)
    remain2 = remain * remain
    return ((remain2 * remain2) * (1.25 - remain)).astype(bf16)


def bin_kernel(live_ref, entries_ref, count_ref, after_ref, bins_ref):
    live = live_ref[0]

    def step(i, carry):
        entries = [entries_ref[i * 16 + u] for u in range(16)]
        for entry in entries:
            bins_ref[entry >> 16] = entry
        return carry

    def last(e, carry):
        entry = entries_ref[e]
        bins_ref[entry >> 16] = entry
        return carry

    groups = live >> 4
    lax.fori_loop(0, groups, step, 0)
    lax.fori_loop(groups * 16, live, last, 0)
    for part in range(3):
        for j in range(TAIL):
            bins_ref[part * LIST + count_ref[part] + j] = 0


def spread(strip, t):
    return jnp.broadcast_to(strip[:, t : t + 1], (TILE, TILE))


def row_kernel(own_ref, near_ref, px, py, own_out):
    def row_prepare(r, carry):
        strip = near_ref[r, 256:272, :].astype(f32).T
        for t in range(8):
            px[r * 8 + t] = spread(strip, t)
            py[r * 8 + t] = spread(strip, 8 + t)
        return carry

    lax.fori_loop(0, 8, row_prepare, 0)
    where = own_ref[256:272, :].astype(f32)
    strip = where.T
    for t in range(8):
        dx = spread(strip, t) - where[t : t + 1]
        dy = spread(strip, 8 + t) - where[8 + t : 9 + t]
        block = radial(dx * dx + dy * dy)
        own_out[:, t * TILE : (t + 1) * TILE] = KERNEL_SCALE * lax.dot_general(
            own_ref[t * 32 : (t + 1) * 32, :], block, NT, preferred_element_type=f32
        )


def z_slot(distance):
    low, high = distance & 3, distance >> 2
    return (low << 1) + (high ^ (low & (low >> 1)))


def part_kernel(part, place_ref, count_ref, bins_ref, near_ref, px, py, col_ref, *refs):
    if part == 0:
        row_acc, *col_out, qx, qy, col_acc = refs
        row_acc[...] = jnp.zeros_like(row_acc)
    elif part == 1:
        before, row_acc, *col_out, qx, qy, col_acc = refs
        row_acc[...] = before[...]
    else:
        before, row_acc, row_out, *col_out, qx, qy, col_acc = refs
        row_acc[...] = before[...]
    z_own = place_ref[0]
    live = count_ref[part]
    col_acc[...] = jnp.zeros_like(col_acc)

    def col_prepare(r, carry):
        where = col_ref[r, 256:272, :].astype(f32)
        for t in range(8):
            qx[r * 8 + t] = jnp.broadcast_to(where[t : t + 1], (8, TILE))
            qy[r * 8 + t] = jnp.broadcast_to(where[8 + t : 9 + t], (8, TILE))
        return carry

    lax.fori_loop(0, 8 * PARTS[part], col_prepare, 0)

    def several(start, size, masked):
        results = []
        for u in range(size):
            e = start + u
            entry = bins_ref[part * LIST + e]
            a, b = entry & 255, (entry >> 8) & 255
            near = near_ref[a >> 3, pl.ds(pl.multiple_of((a & 7) * 32, 32), 32), :]
            far = col_ref[b >> 3, pl.ds(pl.multiple_of((b & 7) * 32, 32), 32), :]
            if masked:
                keep = jnp.where(e < live, 1.0, 0.0).astype(bf16)
                near, far = near * keep, far * keep
            dx = px[a].reshape(16, 8, TILE) - qx[b][None]
            dy = py[a].reshape(16, 8, TILE) - qy[b][None]
            block = radial((dx * dx + dy * dy).reshape(TILE, TILE))
            forward = lax.dot_general(far, block, NT, preferred_element_type=f32)
            backward = lax.dot_general(near, block, NN, preferred_element_type=f32)
            results.append((a, b, forward, backward))
        for a, b, forward, backward in results:
            row_acc[a] += forward
            col_acc[b] += backward

    whole = live // UNROLL

    def body(i, carry):
        several(i * UNROLL, UNROLL, False)
        return carry

    def tail(i, carry):
        several(whole * UNROLL + i * TAIL, TAIL, True)
        return carry

    lax.fori_loop(0, whole, body, 0)
    lax.fori_loop(0, (live - whole * UNROLL + TAIL - 1) // TAIL, tail, 0)

    def finish(z, carry):
        for k in range(PARTS[part]):
            for t in range(8):
                total = KERNEL_SCALE * col_acc[k * 64 + z_slot(z) * 8 + t]
                col_out[k][(z_own - z) & 7, t * 32 : (t + 1) * 32, :] = total.astype(bf16)
        return carry

    lax.fori_loop(0, 8, finish, 0)
    if part == 2:

        def finish_row(r, carry):
            for t in range(8):
                row_out[r, t * 32 : (t + 1) * 32, :] = (KERNEL_SCALE * row_acc[r * 8 + t]).astype(bf16)
            return carry

        lax.fori_loop(0, 8, finish_row, 0)


def add_kernel(own, below, far, above, out):
    for z in range(8):
        total = (own[z].astype(f32) + below[z].astype(f32)) + (far[z].astype(f32) + above[z].astype(f32))
        out[z] = total.astype(bf16)


def dot32(former, latter, dims):
    return lax.dot_general(former, latter, dims, precision=HIGHEST, preferred_element_type=f32)


def gram_kernel(direction_ref, residual_ref, own_ref, row_ref, col_ref, image_ref, gram_ref):
    for t in range(8):
        here = slice(t * 32, (t + 1) * 32)
        lanes = slice(t * TILE, (t + 1) * TILE)
        total = NUGGET * direction_ref[:, lanes] + own_ref[:, lanes]
        for part in range(row_ref.shape[0]):
            total = total + row_ref[part, here, :].astype(f32)
        for part in range(col_ref.shape[0]):
            total = total + col_ref[part, here, :].astype(f32)
        image_ref[:, lanes] = total
    direction, residual, image = direction_ref[...], residual_ref[...], image_ref[...]
    gram_ref[0:32, 0:32] = dot32(direction, image, NT)
    gram_ref[0:32, 32:64] = dot32(direction, residual, NT)
    gram_ref[0:32, 64:96] = dot32(residual, residual, NT)
    gram_ref[0:32, 96:128] = dot32(residual, image, NT)
    square = dot32(image, image, NT)
    for t in range(4):
        gram_ref[32:40, t * 32 : (t + 1) * 32] = square[t * 8 : (t + 1) * 8]


def solve_kernel(gram_ref, solution_ref, residual_ref, direction_ref, image_ref, solution_out, residual_out, direction_out):
    gram = gram_ref[...]
    curvature, crossing = gram[0:32, 0:32], gram[0:32, 32:64]
    norm_old, mixed = gram[0:32, 64:96], gram[0:32, 96:128]
    square = jnp.concatenate([gram[32:40, t * 32 : (t + 1) * 32] for t in range(4)], 0)
    row = lax.broadcasted_iota(jnp.int32, (32, 64), 0)
    lane = lax.broadcasted_iota(jnp.int32, (32, 64), 1)
    unit = jnp.where(row[:, :32] == lane[:, :32], 1.0, 0.0).astype(f32)
    first = jnp.concatenate([0.5 * (curvature + curvature.T), crossing], 1)
    second = jnp.concatenate([0.5 * (norm_old + norm_old.T), unit], 1)

    def eliminate(table, k):
        upper = table[k : k + 1, :] / table[k : k + 1, k : k + 1]
        lower = table[k + 1 : k + 2, :] - table[k + 1 : k + 2, k : k + 1] * upper
        lower = lower / lower[:, k + 1 : k + 2]
        upper = upper - upper[:, k + 1 : k + 2] * lower
        others = table - table[:, k : k + 1] * upper - table[:, k + 1 : k + 2] * lower
        return jnp.where(row == k, upper, jnp.where(row == k + 1, lower, others))

    for k in range(0, 32, 2):
        first, second = eliminate(first, k), eliminate(second, k)
    alpha, inverse = first[:, 32:64], second[:, 32:64]
    cross = dot32(mixed, alpha, NN)
    norm_new = 0.5 * (norm_old + norm_old.T) - cross - cross.T + dot32(alpha, dot32(square, alpha, NN), TN)
    beta = dot32(inverse, norm_new, NN)
    direction = direction_ref[...]
    residual_next = residual_ref[...] - dot32(alpha, image_ref[...], TN)
    residual_out[...] = residual_next
    solution_out[...] = solution_ref[...] + dot32(alpha, direction, TN)
    direction_out[...] = residual_next + dot32(beta, direction, TN)


def shifts(value, axis, size):
    return [lax.ppermute(value, axis, [(i, (i + k) % size) for i in range(size)]) for k in range(1, size)]


def swap(value):
    return lax.ppermute(value, "core", [(0, 1), (1, 0)])


def on_device(solution_field, residual, direction, positions, tile_pairs, pair_count):
    shape = jax.ShapeDtypeStruct
    own_points = direction.shape[1]
    packed = pl.pallas_call(
        pack_kernel, out_shape=shape((272, TILE), bf16), in_specs=[VMEM] * 2, out_specs=VMEM, compiler_params=SMALL, name="pack"
    )(direction, positions)
    def moved(value, axis, size, shift):
        return lax.ppermute(value, axis, [(i, (i + shift) % size) for i in range(size)])

    row_half = jnp.stack([packed] + shifts(packed, "y", 4))
    pair = jnp.stack([packed, moved(packed, "z", 8, 4)])
    one, two, back = [moved(pair, "z", 8, shift) for shift in (1, 2, -1)]
    pair_below, pair_above = moved(pair, "x", 4, 1), moved(pair, "x", 4, -1)
    rest = jnp.concatenate([one, two, back], 0)
    row_half, rest = lax.optimization_barrier((row_half, rest))
    rest_below, rest_above = moved(rest, "x", 4, 1), moved(rest, "x", 4, -1)
    row_all = jnp.concatenate([row_half, swap(row_half)], 0)
    x_own, y_own, z_own, core_own = [lax.axis_index(name).astype(jnp.int32) for name in ("x", "y", "z", "core")]
    place = z_own.reshape(1)
    tile_pairs, counted, pair_above, row_half = lax.optimization_barrier((tile_pairs, pair_count, pair_above, row_half))
    a, b = tile_pairs[0], tile_pairs[1]
    near_slot = ((y_own - (a >> 4)) & 3) + ((((a >> 3) & 1) ^ core_own) << 2)
    x_far = (x_own - (b >> 3)) & 3
    far_slot = z_slot((z_own - (b >> 5)) & 7) + jnp.where(x_far == 3, 8, 0)
    entries = (near_slot << 3) + (a & 7) + (far_slot << 11) + ((b & 7) << 8)
    part = jnp.where(x_far == 2, 1, jnp.where(x_far == 0, 2, 0))
    part = jnp.where(jnp.arange(part.shape[0], dtype=jnp.int32) < counted[0], part, 3).reshape(-1, TILE)
    hot = (part[None] == jnp.arange(3, dtype=jnp.int32)[:, None, None]).astype(bf16)
    ahead = jnp.triu(jnp.ones((TILE, TILE), bf16), 1)
    rows = hot.shape[1]
    ahead_row = jnp.einsum("prl,lm->prm", hot, ahead, preferred_element_type=f32)
    row_count = jnp.sum(hot.astype(f32), 2)
    ahead_rows = jnp.sum(row_count[:, :, None] * jnp.triu(jnp.ones((rows, rows), f32), 1)[None], 1)
    spot = ahead_row + ahead_rows[:, :, None] + (jnp.arange(3, dtype=jnp.int32) * LIST).astype(f32)[:, None, None]
    spot = jnp.sum(hot.astype(f32) * spot, 0).astype(jnp.int32).reshape(-1)
    entries = entries + (spot << 16)
    counts = jnp.sum(row_count, 1).astype(jnp.int32)
    bins = pl.pallas_call(
        bin_kernel,
        out_shape=shape((3 * LIST,), jnp.int32),
        in_specs=[SMEM, SMEM, SMEM, VMEM],
        out_specs=SMEM,
        compiler_params=SMALL,
        name="bins",
    )(pair_count, entries, counts, pair_above[0, :16])
    spread_shape = shape((64, TILE, TILE), f32)
    px, py, own_product = pl.pallas_call(
        row_kernel,
        out_shape=(spread_shape, spread_shape, shape((PROBES, own_points), f32)),
        in_specs=[VMEM] * 2,
        out_specs=(VMEM,) * 3,
        compiler_params=PARAMS,
        name="rows",
    )(packed, row_all)
    rest_below, rest_above, bins, px = lax.optimization_barrier((rest_below, rest_above, bins, px))
    far_below = moved(jnp.concatenate([pair_below[:1], rest_below[:3]], 0), "x", 4, 1)
    far_above = moved(jnp.concatenate([pair_above[1:], rest_above[3:]], 0), "x", 4, -1)
    columns = (
        jnp.concatenate([pair_below, rest_below, pair_above, rest_above], 0),
        jnp.concatenate([far_below[:1], far_above[:1], far_below[1:], far_above[1:]], 0),
        jnp.concatenate([pair, rest], 0),
    )
    acc = shape((64, PROBES, TILE), f32)
    block = shape((8, 256, TILE), bf16)

    def pairs(part, totals=None):
        tiles = PARTS[part] * 64
        outs = (acc,) + (block,) * (PARTS[part] + (part == 2))
        operands = (place, counts, bins, row_all, px, py, columns[part]) + (() if part == 0 else (totals,))
        return pl.pallas_call(
            functools.partial(part_kernel, part),
            out_shape=outs,
            in_specs=[SMEM] * 3 + [VMEM] * (len(operands) - 3),
            out_specs=(VMEM,) * len(outs),
            scratch_shapes=[pltpu.VMEM((tiles, 8, TILE), f32)] * 2 + [pltpu.VMEM((tiles, PROBES, TILE), f32)],
            input_output_aliases={} if part == 0 else {7: 0},
            compiler_params=PARAMS,
            name="pairs",
        )(*operands)

    totals, for_below, for_above = pairs(0)
    below, above = moved(for_below, "x", 4, -1), moved(for_above, "x", 4, 1)
    totals, for_far = pairs(1, totals)
    far = moved(for_far, "x", 4, 2)
    totals, row_sum, own = pairs(2, totals)
    sums = pl.pallas_call(
        add_kernel,
        out_shape=block,
        in_specs=[VMEM] * 4,
        out_specs=VMEM,
        compiler_params=PARAMS,
        name="add",
    )(own, below, far, above)
    col_parts = lax.all_to_all(sums, "z", 0, 0)
    half = (row_sum[:4].astype(f32) + swap(row_sum[4:]).astype(f32)).astype(bf16)
    row_parts = [half[0]] + [
        lax.ppermute(half[k], "y", [(i, (i - k) % 4) for i in range(4)]) for k in range(1, 4)
    ]
    row_parts = jnp.stack(row_parts)
    image, gram = pl.pallas_call(
        gram_kernel,
        out_shape=(shape((PROBES, own_points), f32), shape((40, TILE), f32)),
        in_specs=[VMEM] * 5,
        out_specs=(VMEM, VMEM),
        compiler_params=PARAMS,
        name="gram",
    )(direction, residual, own_product, row_parts, col_parts)
    gram = gram + swap(gram)
    gram = sum(shifts(gram, "y", 4), gram)
    gram = sum(shifts(gram, "x", 4), gram)
    gram = gram + lax.ppermute(gram, "z", [(i, (i + 4) % 8) for i in range(8)])
    gram = sum(shifts(gram, "z", 8)[:3], gram)
    return pl.pallas_call(
        solve_kernel,
        out_shape=(shape((PROBES, own_points), f32),) * 3,
        in_specs=[VMEM] * 5,
        out_specs=(VMEM,) * 3,
        compiler_params=PARAMS,
        name="solve",
    )(gram, solution_field, residual, direction, image)


def solution(mesh):
    fine = Mesh(np.asarray(mesh.devices).reshape(8, 4, 4, 2), ("z", "x", "y", "core"))
    points = P(None, ("z", "x", "y", "core"))
    return jax.shard_map(
        on_device,
        mesh=fine,
        in_specs=(points,) * 5 + (P(("z", "x", "y", "core")),),
        out_specs=(points,) * 3,
        check_vma=False,
    )
```

```python
import functools

import jax
import jax.numpy as jnp
import numpy as np
from jax import lax
from jax.experimental import pallas as pl
from jax.experimental.pallas import tpu as pltpu
from jax.sharding import Mesh
from jax.sharding import PartitionSpec as P

TILE = 128
PROBES = 32
UNROLL = 32
TAIL = 8
PARTS = (2, 1, 1)
LIST = 1536 + UNROLL
NUGGET = 2.0
KERNEL_SCALE = 0.1
HIGHEST = lax.Precision.HIGHEST
f32, bf16 = jnp.float32, jnp.bfloat16
VMEM = pl.BlockSpec(memory_space=pltpu.VMEM)
SMEM = pl.BlockSpec(memory_space=pltpu.SMEM)
NT = (((1,), (1,)), ((), ()))
NN = (((1,), (0,)), ((), ()))
TN = (((0,), (0,)), ((), ()))
PARAMS = pltpu.CompilerParams(vmem_limit_bytes=16 * 2**20)
SMALL = pltpu.CompilerParams(vmem_limit_bytes=4 * 2**20)


def pack_kernel(direction_in, positions_in, packed_ref, direction_ref, positions_ref, sems):
    copies = [
        pltpu.make_async_copy(direction_in, direction_ref, sems.at[0]),
        pltpu.make_async_copy(positions_in, positions_ref, sems.at[1]),
    ]
    for copy in copies:
        copy.start()
    for copy in copies:
        copy.wait()
    for t in range(8):
        packed_ref[t * 32 : (t + 1) * 32, :] = direction_ref[:, t * TILE : (t + 1) * TILE].astype(bf16)
    where = positions_ref[...].astype(f32)
    rows = [where[d : d + 1, t * TILE : (t + 1) * TILE] for d in range(2) for t in range(8)]
    packed_ref[256:272, :] = jnp.concatenate(rows, 0).astype(bf16)


def radial(square):
    distance = pl.reciprocal(lax.rsqrt(square), approx=True)
    remain = jnp.maximum(1.0 - distance, 0.0)
    remain2 = remain * remain
    return ((remain2 * remain2) * (1.25 - remain)).astype(bf16)


def bin_kernel(live_ref, entries_ref, count_ref, after_ref, bins_ref):
    live = live_ref[0]

    def step(i, carry):
        entries = [entries_ref[i * 16 + u] for u in range(16)]
        for entry in entries:
            bins_ref[entry >> 16] = entry
        return carry

    def last(e, carry):
        entry = entries_ref[e]
        bins_ref[entry >> 16] = entry
        return carry

    groups = live >> 4
    lax.fori_loop(0, groups, step, 0)
    lax.fori_loop(groups * 16, live, last, 0)
    for part in range(3):
        for j in range(TAIL):
            bins_ref[part * LIST + count_ref[part] + j] = 0


def spread(strip, t):
    return jnp.broadcast_to(strip[:, t : t + 1], (TILE, TILE))


def row_kernel(own_ref, near_ref, px, py, own_out):
    def row_prepare(r, carry):
        strip = near_ref[r, 256:272, :].astype(f32).T
        for t in range(8):
            px[r * 8 + t] = spread(strip, t)
            py[r * 8 + t] = spread(strip, 8 + t)
        return carry

    lax.fori_loop(0, 8, row_prepare, 0)
    where = own_ref[256:272, :].astype(f32)
    strip = where.T
    for t in range(8):
        dx = spread(strip, t) - where[t : t + 1]
        dy = spread(strip, 8 + t) - where[8 + t : 9 + t]
        block = radial(dx * dx + dy * dy)
        own_out[:, t * TILE : (t + 1) * TILE] = KERNEL_SCALE * lax.dot_general(
            own_ref[t * 32 : (t + 1) * 32, :], block, NT, preferred_element_type=f32
        )


def z_slot(distance):
    low, high = distance & 3, distance >> 2
    return (low << 1) + (high ^ (low & (low >> 1)))


def part_kernel(part, place_ref, count_ref, bins_ref, near_ref, px, py, col_ref, *refs):
    if part == 0:
        row_acc, *col_out, qx, qy, col_acc = refs
        row_acc[...] = jnp.zeros_like(row_acc)
    elif part == 1:
        before, row_acc, *col_out, qx, qy, col_acc = refs
        row_acc[...] = before[...]
    else:
        before, row_acc, row_out, *col_out, qx, qy, col_acc = refs
        row_acc[...] = before[...]
    z_own = place_ref[0]
    live = count_ref[part]
    col_acc[...] = jnp.zeros_like(col_acc)

    def col_prepare(r, carry):
        where = col_ref[r, 256:272, :].astype(f32)
        for t in range(8):
            qx[r * 8 + t] = jnp.broadcast_to(where[t : t + 1], (8, TILE))
            qy[r * 8 + t] = jnp.broadcast_to(where[8 + t : 9 + t], (8, TILE))
        return carry

    lax.fori_loop(0, 8 * PARTS[part], col_prepare, 0)

    def several(start, size, masked):
        results = []
        for u in range(size):
            e = start + u
            entry = bins_ref[part * LIST + e]
            a, b = entry & 255, (entry >> 8) & 255
            near = near_ref[a >> 3, pl.ds(pl.multiple_of((a & 7) * 32, 32), 32), :]
            far = col_ref[b >> 3, pl.ds(pl.multiple_of((b & 7) * 32, 32), 32), :]
            if masked:
                keep = jnp.where(e < live, 1.0, 0.0).astype(bf16)
                near, far = near * keep, far * keep
            dx = px[a].reshape(16, 8, TILE) - qx[b][None]
            dy = py[a].reshape(16, 8, TILE) - qy[b][None]
            block = radial((dx * dx + dy * dy).reshape(TILE, TILE))
            forward = lax.dot_general(far, block, NT, preferred_element_type=f32)
            backward = lax.dot_general(near, block, NN, preferred_element_type=f32)
            results.append((a, b, forward, backward))
        for a, b, forward, backward in results:
            row_acc[a] += forward
            col_acc[b] += backward

    whole = live // UNROLL

    def body(i, carry):
        several(i * UNROLL, UNROLL, False)
        return carry

    def tail(i, carry):
        several(whole * UNROLL + i * TAIL, TAIL, True)
        return carry

    lax.fori_loop(0, whole, body, 0)
    lax.fori_loop(0, (live - whole * UNROLL + TAIL - 1) // TAIL, tail, 0)

    def finish(z, carry):
        for k in range(PARTS[part]):
            for t in range(8):
                total = KERNEL_SCALE * col_acc[k * 64 + z_slot(z) * 8 + t]
                col_out[k][(z_own - z) & 7, t * 32 : (t + 1) * 32, :] = total.astype(bf16)
        return carry

    lax.fori_loop(0, 8, finish, 0)
    if part == 2:

        def finish_row(r, carry):
            for t in range(8):
                row_out[r, t * 32 : (t + 1) * 32, :] = (KERNEL_SCALE * row_acc[r * 8 + t]).astype(bf16)
            return carry

        lax.fori_loop(0, 8, finish_row, 0)


def add_kernel(own, below, far, above, out):
    for z in range(8):
        total = (own[z].astype(f32) + below[z].astype(f32)) + (far[z].astype(f32) + above[z].astype(f32))
        out[z] = total.astype(bf16)


def dot32(former, latter, dims):
    return lax.dot_general(former, latter, dims, precision=HIGHEST, preferred_element_type=f32)


def gram_kernel(direction_ref, residual_ref, own_ref, row_ref, col_ref, image_ref, gram_ref):
    for t in range(8):
        here = slice(t * 32, (t + 1) * 32)
        lanes = slice(t * TILE, (t + 1) * TILE)
        total = NUGGET * direction_ref[:, lanes] + own_ref[:, lanes]
        for part in range(row_ref.shape[0]):
            total = total + row_ref[part, here, :].astype(f32)
        for part in range(col_ref.shape[0]):
            total = total + col_ref[part, here, :].astype(f32)
        image_ref[:, lanes] = total
    direction, residual, image = direction_ref[...], residual_ref[...], image_ref[...]
    gram_ref[0:32, 0:32] = dot32(direction, image, NT)
    gram_ref[0:32, 32:64] = dot32(direction, residual, NT)
    gram_ref[0:32, 64:96] = dot32(residual, residual, NT)
    gram_ref[0:32, 96:128] = dot32(residual, image, NT)
    square = dot32(image, image, NT)
    for t in range(4):
        gram_ref[32:40, t * 32 : (t + 1) * 32] = square[t * 8 : (t + 1) * 8]


def solve_kernel(gram_ref, solution_ref, residual_ref, direction_ref, image_ref, solution_out, residual_out, direction_out):
    gram = gram_ref[...]
    curvature, crossing = gram[0:32, 0:32], gram[0:32, 32:64]
    norm_old, mixed = gram[0:32, 64:96], gram[0:32, 96:128]
    square = jnp.concatenate([gram[32:40, t * 32 : (t + 1) * 32] for t in range(4)], 0)
    row = lax.broadcasted_iota(jnp.int32, (32, 64), 0)
    lane = lax.broadcasted_iota(jnp.int32, (32, 64), 1)
    unit = jnp.where(row[:, :32] == lane[:, :32], 1.0, 0.0).astype(f32)
    first = jnp.concatenate([0.5 * (curvature + curvature.T), crossing], 1)
    second = jnp.concatenate([0.5 * (norm_old + norm_old.T), unit], 1)

    def eliminate(table, k):
        pivot_row = table[k : k + 1, :] / table[k : k + 1, k : k + 1]
        return jnp.where(row == k, pivot_row, table - table[:, k : k + 1] * pivot_row)

    for k in range(32):
        first, second = eliminate(first, k), eliminate(second, k)
    alpha, inverse = first[:, 32:64], second[:, 32:64]
    cross = dot32(mixed, alpha, NN)
    norm_new = 0.5 * (norm_old + norm_old.T) - cross - cross.T + dot32(alpha, dot32(square, alpha, NN), TN)
    beta = dot32(inverse, norm_new, NN)
    direction = direction_ref[...]
    residual_next = residual_ref[...] - dot32(alpha, image_ref[...], TN)
    residual_out[...] = residual_next
    solution_out[...] = solution_ref[...] + dot32(alpha, direction, TN)
    direction_out[...] = residual_next + dot32(beta, direction, TN)


def shifts(value, axis, size):
    return [lax.ppermute(value, axis, [(i, (i + k) % size) for i in range(size)]) for k in range(1, size)]


def swap(value):
    return lax.ppermute(value, "core", [(0, 1), (1, 0)])


def on_device(solution_field, residual, direction, positions, tile_pairs, pair_count):
    shape = jax.ShapeDtypeStruct
    own_points = direction.shape[1]
    packed = pl.pallas_call(
        pack_kernel,
        out_shape=shape((272, TILE), bf16),
        in_specs=[pl.BlockSpec(memory_space=pl.ANY)] * 2,
        out_specs=VMEM,
        scratch_shapes=[
            pltpu.VMEM((PROBES, own_points), f32),
            pltpu.VMEM((2, own_points), bf16),
            pltpu.SemaphoreType.DMA((2,)),
        ],
        compiler_params=SMALL,
        name="pack",
    )(direction, positions)
    def moved(value, axis, size, shift):
        return lax.ppermute(value, axis, [(i, (i + shift) % size) for i in range(size)])

    row_half = jnp.stack([packed] + shifts(packed, "y", 4))
    pair = jnp.stack([packed, moved(packed, "z", 8, 4)])
    one, two, back = [moved(pair, "z", 8, shift) for shift in (1, 2, -1)]
    pair_below, pair_above = moved(pair, "x", 4, 1), moved(pair, "x", 4, -1)
    rest = jnp.concatenate([one, two, back], 0)
    row_half, rest = lax.optimization_barrier((row_half, rest))
    rest_below, rest_above = moved(rest, "x", 4, 1), moved(rest, "x", 4, -1)
    row_all = jnp.concatenate([row_half, swap(row_half)], 0)
    x_own, y_own, z_own, core_own = [lax.axis_index(name).astype(jnp.int32) for name in ("x", "y", "z", "core")]
    place = z_own.reshape(1)
    tile_pairs, counted, pair_above, row_half = lax.optimization_barrier((tile_pairs, pair_count, pair_above, row_half))
    a, b = tile_pairs[0], tile_pairs[1]
    near_slot = ((y_own - (a >> 4)) & 3) + ((((a >> 3) & 1) ^ core_own) << 2)
    x_far = (x_own - (b >> 3)) & 3
    far_slot = z_slot((z_own - (b >> 5)) & 7) + jnp.where(x_far == 3, 8, 0)
    entries = (near_slot << 3) + (a & 7) + (far_slot << 11) + ((b & 7) << 8)
    part = jnp.where(x_far == 2, 1, jnp.where(x_far == 0, 2, 0))
    part = jnp.where(jnp.arange(part.shape[0], dtype=jnp.int32) < counted[0], part, 3).reshape(-1, TILE)
    hot = (part[None] == jnp.arange(3, dtype=jnp.int32)[:, None, None]).astype(bf16)
    ahead = jnp.triu(jnp.ones((TILE, TILE), bf16), 1)
    rows = hot.shape[1]
    ahead_row = jnp.einsum("prl,lm->prm", hot, ahead, preferred_element_type=f32)
    row_count = jnp.sum(hot.astype(f32), 2)
    ahead_rows = jnp.sum(row_count[:, :, None] * jnp.triu(jnp.ones((rows, rows), f32), 1)[None], 1)
    spot = ahead_row + ahead_rows[:, :, None] + (jnp.arange(3, dtype=jnp.int32) * LIST).astype(f32)[:, None, None]
    spot = jnp.sum(hot.astype(f32) * spot, 0).astype(jnp.int32).reshape(-1)
    entries = entries + (spot << 16)
    counts = jnp.sum(row_count, 1).astype(jnp.int32)
    bins = pl.pallas_call(
        bin_kernel,
        out_shape=shape((3 * LIST,), jnp.int32),
        in_specs=[SMEM, SMEM, SMEM, VMEM],
        out_specs=SMEM,
        compiler_params=SMALL,
        name="bins",
    )(pair_count, entries, counts, pair_above[0, :16])
    spread_shape = shape((64, TILE, TILE), f32)
    px, py, own_product = pl.pallas_call(
        row_kernel,
        out_shape=(spread_shape, spread_shape, shape((PROBES, own_points), f32)),
        in_specs=[VMEM] * 2,
        out_specs=(VMEM,) * 3,
        compiler_params=PARAMS,
        name="rows",
    )(packed, row_all)
    rest_below, rest_above, bins, px = lax.optimization_barrier((rest_below, rest_above, bins, px))
    far_below = moved(jnp.concatenate([pair_below[:1], rest_below[:3]], 0), "x", 4, 1)
    far_above = moved(jnp.concatenate([pair_above[1:], rest_above[3:]], 0), "x", 4, -1)
    columns = (
        jnp.concatenate([pair_below, rest_below, pair_above, rest_above], 0),
        jnp.concatenate([far_below[:1], far_above[:1], far_below[1:], far_above[1:]], 0),
        jnp.concatenate([pair, rest], 0),
    )
    acc = shape((64, PROBES, TILE), f32)
    block = shape((8, 256, TILE), bf16)

    def pairs(part, totals=None):
        tiles = PARTS[part] * 64
        outs = (acc,) + (block,) * (PARTS[part] + (part == 2))
        operands = (place, counts, bins, row_all, px, py, columns[part]) + (() if part == 0 else (totals,))
        return pl.pallas_call(
            functools.partial(part_kernel, part),
            out_shape=outs,
            in_specs=[SMEM] * 3 + [VMEM] * (len(operands) - 3),
            out_specs=(VMEM,) * len(outs),
            scratch_shapes=[pltpu.VMEM((tiles, 8, TILE), f32)] * 2 + [pltpu.VMEM((tiles, PROBES, TILE), f32)],
            input_output_aliases={} if part == 0 else {7: 0},
            compiler_params=PARAMS,
            name="pairs",
        )(*operands)

    totals, for_below, for_above = pairs(0)
    below, above = moved(for_below, "x", 4, -1), moved(for_above, "x", 4, 1)
    totals, for_far = pairs(1, totals)
    far = moved(for_far, "x", 4, 2)
    totals, row_sum, own = pairs(2, totals)
    sums = pl.pallas_call(
        add_kernel,
        out_shape=block,
        in_specs=[VMEM] * 4,
        out_specs=VMEM,
        compiler_params=PARAMS,
        name="add",
    )(own, below, far, above)
    col_parts = lax.all_to_all(sums, "z", 0, 0)
    half = (row_sum[:4].astype(f32) + swap(row_sum[4:]).astype(f32)).astype(bf16)
    row_parts = [half[0]] + [
        lax.ppermute(half[k], "y", [(i, (i - k) % 4) for i in range(4)]) for k in range(1, 4)
    ]
    row_parts = jnp.stack(row_parts)
    image, gram = pl.pallas_call(
        gram_kernel,
        out_shape=(shape((PROBES, own_points), f32), shape((40, TILE), f32)),
        in_specs=[VMEM] * 5,
        out_specs=(VMEM, VMEM),
        compiler_params=PARAMS,
        name="gram",
    )(direction, residual, own_product, row_parts, col_parts)
    gram = gram + swap(gram)
    gram = sum(shifts(gram, "y", 4), gram)
    gram = sum(shifts(gram, "x", 4), gram)
    gram = gram + lax.ppermute(gram, "z", [(i, (i + 4) % 8) for i in range(8)])
    gram = sum(shifts(gram, "z", 8)[:3], gram)
    return pl.pallas_call(
        solve_kernel,
        out_shape=(shape((PROBES, own_points), f32),) * 3,
        in_specs=[VMEM] * 5,
        out_specs=(VMEM,) * 3,
        compiler_params=PARAMS,
        name="solve",
    )(gram, solution_field, residual, direction, image)


def solution(mesh):
    fine = Mesh(np.asarray(mesh.devices).reshape(8, 4, 4, 2), ("z", "x", "y", "core"))
    points = P(None, ("z", "x", "y", "core"))
    return jax.shard_map(
        on_device,
        mesh=fine,
        in_specs=(points,) * 5 + (P(("z", "x", "y", "core")),),
        out_specs=(points,) * 3,
        check_vma=False,
    )
```
